32 devices in a mesh: sensor: 16 (over z, y, x), tm: 2 (over core).
Axes of the slice: x: 2, y: 2, z: 4, core: 2. Of those that a mesh axis runs over, the one named last changes fastest.
Arguments:
- inputs: bfloat16 [1024, 32, 128], P('sensor', 'tm'), may hold values from -6 to 6
- mask: int32 [1024, 32], P('sensor', 'tm'), may hold values 0 or 1
- projector: float32 [64, 128], replicated, may hold values from -6 to 6
- w_key: bfloat16 [128, 128], replicated, may hold values from -0.5 to 0.5
- w_value: bfloat16 [128, 128], replicated, may hold values from -0.5 to 0.5
- w_query: bfloat16 [128, 128], replicated, may hold values from -0.5 to 0.5
- w_out: bfloat16 [128, 128], replicated, may hold values from -0.5 to 0.5
- cotangent: bfloat16 [1024, 32, 128], P('sensor', 'tm'), may hold values from -6 to 6
Outputs:
- layer_out: bfloat16 [1024, 32, 128], P('sensor', 'tm')
- grad_inputs: bfloat16 [1024, 32, 128], P('sensor', 'tm')
- grad_projector: float32 [64, 128], P('tm')
- grad_key: float32 [128, 128], P('tm')
- grad_value: float32 [128, 128], P('tm')
- grad_query: float32 [128, 128], P('tm')
- grad_out: float32 [128, 128], P('tm')
The draws below stay inside these ranges and needn't reach their ends.
All inputs are finite; a program needn't handle non-finite values. No bound on the sum of `mask` on one device may be relied on, other than what follows from the above.
Results may differ from the reference program's by a relative error of at most 0.0095.
Values sent between devices are 32-bit elements; how exact they have to be, the bound alone decides.
No kernel may reach another device: no remote copies, remote signals or barrier semaphores. Data moves between devices by JAX's collectives and lax.ppermute only.
A program may use at most 64 MiB of HBM per device.

```python
import jax
import jax.numpy as jnp
from jax import lax

D = 128
K = 64
SENSORS = 1024
STEPS = 32


def touch_ends(values, own_key, least, top_value):
    longest = values.shape.index(max(values.shape))
    spots = []
    for shift in (0, 1):
        where = [jax.random.randint(jax.random.fold_in(own_key, axis), (), 0, length) for axis, length in enumerate(values.shape)]
        where[longest] = (where[longest] + shift) % values.shape[longest]
        spots.append(tuple(where))
    return values.at[spots[0]].set(least).at[spots[1]].set(top_value)


def steps_of(own_key, extent, split, least, top_value):
    gain, own = 1.0, jax.random.fold_in(own_key, 6)
    for position, parts in split:
        heights = jnp.exp(jax.random.uniform(jax.random.fold_in(own, position), (parts,), jnp.float32, least / len(split), top_value / len(split)))
        gain = gain * jnp.repeat(heights, extent[position] // parts).reshape([-1 if axis == position else 1 for axis in range(len(extent))])
    return gain


def noise(rng, shape, deviation, limit, pieces=(), kind=jnp.bfloat16):
    drawn = deviation * jax.random.normal(rng, shape, jnp.float32)
    if pieces:
        drawn = drawn * steps_of(rng, shape, pieces, -0.22, 0.18)
    return jnp.clip(drawn, -limit, limit).astype(kind)


def setup_inputs(seed: int = 0) -> dict:
    keys = jax.random.split(jax.random.key(seed), 9)
    inputs = noise(keys[0], (SENSORS, STEPS, D), 1.0, 6.0, ((0, 16), (1, 2)))
    mask = touch_ends((jax.random.randint(keys[1], (SENSORS, STEPS), 0, 4) < 3).astype(jnp.int32), jax.random.fold_in(keys[1], 1), 0, 1)
    projector = noise(keys[2], (K, D), 1.0, 6.0, (), jnp.float32)
    w_key = noise(keys[3], (D, D), D ** -0.5, 0.5)
    w_value = noise(keys[4], (D, D), D ** -0.5, 0.5)
    w_query = noise(keys[5], (D, D), D ** -0.5, 0.5)
    w_out = noise(keys[6], (D, D), D ** -0.5, 0.5)
    cotangent = noise(keys[7], (SENSORS, STEPS, D), 1.0, 6.0, ((0, 16), (1, 2)))
    return {"inputs": inputs, "mask": mask, "projector": projector, "w_key": w_key, "w_value": w_value, "w_query": w_query, "w_out": w_out, "cotangent": cotangent}


sharpness_divisor = 12.0
epsilon = 1e-06
largest_energy = lax.Precision.HIGHEST

def normalize(vector):
    return vector * lax.rsqrt(lax.optimization_barrier(jnp.mean(vector * vector, axis=-1, keepdims=True)) + epsilon)

def attend_in(matched_plain_vector, values, projector):
    matched_unit_vector = normalize(matched_plain_vector)
    mapping_unit_vector = normalize(projector)
    attention_energies = sharpness_divisor / matched_plain_vector.shape[-1] * jnp.dot(mapping_unit_vector, matched_unit_vector.T, precision=largest_energy)
    weights = jnp.exp(attention_energies)
    numerator = jnp.dot(weights, values.astype(jnp.float32), precision=largest_energy)
    denominator = lax.optimization_barrier(jnp.sum(weights, axis=1))
    return (numerator, denominator)

def make_summary(numerator, denominator):
    return numerator / denominator[..., None]

def attend_out(asking_plain_vector, summary):
    asking_unit_vector = normalize(asking_plain_vector)
    pooled_unit_vector = normalize(summary)
    attention_energies = sharpness_divisor / asking_plain_vector.shape[-1] * jnp.dot(asking_unit_vector, pooled_unit_vector.T, precision=largest_energy)
    weights = jnp.exp(attention_energies)
    weights = weights / lax.optimization_barrier(jnp.sum(weights, axis=1, keepdims=True))
    blended = jnp.dot(weights, summary, precision=largest_energy)
    return normalize(blended).astype(jnp.bfloat16)

def contract_rows(left, right):
    return lax.dot_general(left, right, (((0,), (0,)), ((), ())), preferred_element_type=jnp.float32)

def reference(inputs, mask, projector, w_key, w_value, w_query, w_out, cotangent):

    def one_step(totals, slices):
        rows, marks, incoming = slices
        hidden = rows * marks[:, None].astype(rows.dtype)
        matched_plain_vector = jnp.dot(hidden, w_key, preferred_element_type=jnp.float32)
        values = jnp.dot(hidden, w_value, preferred_element_type=jnp.float32).astype(jnp.bfloat16)
        asking_plain_vector = jnp.dot(hidden, w_query, preferred_element_type=jnp.float32)
        (numerator, denominator), in_back = jax.vjp(attend_in, matched_plain_vector, values, projector)
        summary, summary_back = jax.vjp(make_summary, numerator, denominator)
        normed, out_back = jax.vjp(attend_out, asking_plain_vector, summary)
        output_rows = (hidden.astype(jnp.float32) + jnp.dot(normed, w_out, preferred_element_type=jnp.float32)).astype(jnp.bfloat16)
        grad_out = contract_rows(normed, incoming)
        d_normed = jnp.dot(incoming, w_out.T, preferred_element_type=jnp.float32).astype(jnp.bfloat16)
        d_query, d_summary = out_back(d_normed)
        d_numerator, d_denominator = summary_back(d_summary)
        d_key, d_values, d_projector = in_back((d_numerator, d_denominator))
        d_query = d_query.astype(jnp.bfloat16)
        d_key = d_key.astype(jnp.bfloat16)
        grad_key = contract_rows(hidden, d_key)
        grad_value = contract_rows(hidden, d_values)
        grad_query = contract_rows(hidden, d_query)
        d_hidden = incoming.astype(jnp.float32)
        d_hidden = d_hidden + jnp.dot(d_query, w_query.T, preferred_element_type=jnp.float32)
        d_hidden = d_hidden + jnp.dot(d_key, w_key.T, preferred_element_type=jnp.float32)
        d_hidden = d_hidden + jnp.dot(d_values, w_value.T, preferred_element_type=jnp.float32)
        d_inputs = (d_hidden * marks[:, None].astype(jnp.float32)).astype(jnp.bfloat16)
        totals = (totals[0] + d_projector, totals[1] + grad_key, totals[2] + grad_value, totals[3] + grad_query, totals[4] + grad_out)
        return (totals, (output_rows, d_inputs))
    square = jnp.zeros((D, D), jnp.float32)
    start = (jnp.zeros((K, D), jnp.float32), square, square, square, square)
    totals, (outputs, d_inputs) = lax.scan(one_step, start, (jnp.swapaxes(inputs, 0, 1), jnp.swapaxes(mask, 0, 1), jnp.swapaxes(cotangent, 0, 1)))
    return (jnp.swapaxes(outputs, 0, 1), jnp.swapaxes(d_inputs, 0, 1), totals[0], totals[1], totals[2], totals[3], totals[4])
```

```python
import functools
import math

import jax
import jax.numpy as jnp
from jax import lax
from jax.experimental import pallas as pl
from jax.experimental.pallas import tpu as pltpu
from jax.sharding import PartitionSpec as P

sharpness_divisor = 12.0
epsilon = 1e-06
f32 = jnp.float32
bf16 = jnp.bfloat16


def params():
    return pltpu.CompilerParams(vmem_limit_bytes=48 * 1024 * 1024)


def dot(left, right, left_dim, right_dim):
    return lax.dot_general(
        left, right, (((left_dim,), (right_dim,)), ((), ())), preferred_element_type=f32
    )


def rounded_dot(left, right, left_dim, right_dim):
    return dot(left.astype(bf16), right.astype(bf16), left_dim, right_dim)


def inverse_norm(vector):
    return lax.rsqrt(jnp.mean(vector * vector, axis=-1, keepdims=True) + epsilon)


def normalize_back(inverse, unit, gradient):
    return inverse * (gradient - unit * jnp.mean(unit * gradient, axis=-1, keepdims=True))


def outward_kernel(rows_ref, mask_ref, out_ref, wide):
    wide[...] = rows_ref[...].astype(f32)
    marks = None if mask_ref is None else mask_ref[...].astype(f32)
    for t in range(out_ref.shape[0]):
        rows = wide[:, t, :]
        out_ref[t] = rows if marks is None else rows * marks[:, t : t + 1]


def outward(rows, mask):
    sensors, steps, width = rows.shape
    args = (rows,) if mask is None else (rows, mask)
    body = outward_kernel if mask is not None else (lambda r, o, w: outward_kernel(r, None, o, w))
    return pl.pallas_call(
        body,
        out_shape=jax.ShapeDtypeStruct((steps, sensors, width), f32),
        scratch_shapes=[pltpu.VMEM((sensors, steps, width), f32)],
        compiler_params=params(),
    )(*args)


def homeward_kernel(rows_ref, mask_ref, out_ref, wide):
    marks = None if mask_ref is None else mask_ref[...].astype(f32)
    for t in range(rows_ref.shape[0]):
        rows = rows_ref[t]
        wide[:, t, :] = rows if marks is None else rows * marks[:, t : t + 1]
    out_ref[...] = wide[...].astype(out_ref.dtype)


def homeward(rows, mask):
    steps, sensors, width = rows.shape
    args = (rows,) if mask is None else (rows, mask)
    body = homeward_kernel if mask is not None else (lambda r, o, w: homeward_kernel(r, None, o, w))
    return pl.pallas_call(
        body,
        out_shape=jax.ShapeDtypeStruct((sensors, steps, width), bf16),
        scratch_shapes=[pltpu.VMEM((sensors, steps, width), f32)],
        compiler_params=params(),
    )(*args)


def step_rows(ref, t):
    rows = ref[:, t]
    return rows.reshape(rows.shape[0] * rows.shape[1], rows.shape[2])


def project(ref, t, w_key, w_value, w_query):
    hidden = step_rows(ref, t).astype(bf16)
    width = w_key.shape[1]
    both = dot(hidden, jnp.concatenate([w_key, w_value, w_query], axis=1), 1, 0)
    return hidden, both[:, :width], both[:, width : 2 * width].astype(bf16), both[:, 2 * width :]


def scale_of(width):
    return sharpness_divisor / width


def weigh_in(key_raw, projector):
    inverse = inverse_norm(key_raw)
    unit = key_raw * inverse
    mapping = projector * inverse_norm(projector)
    scale = scale_of(key_raw.shape[-1])
    return inverse, unit, jnp.exp(scale * rounded_dot(mapping, unit, 1, 1))


def weigh_out(query_raw, summary):
    inverse = inverse_norm(query_raw)
    unit = query_raw * inverse
    pooled_inverse = inverse_norm(summary)
    pooled = summary * pooled_inverse
    scale = scale_of(query_raw.shape[-1])
    weights = jnp.exp(scale * rounded_dot(pooled, unit, 1, 1))
    attention = weights / jnp.sum(weights, axis=0, keepdims=True)
    return inverse, unit, pooled_inverse, pooled, attention


def in_part(refs, t, num_ref, den_ref):
    hidden, key_raw, values, _ = project(refs["hidden"], t, *refs["projections"])
    _, _, weights = weigh_in(key_raw, refs["projector"])
    num_ref[t] = rounded_dot(weights, values, 1, 0)
    den_ref[t] = jnp.broadcast_to(jnp.sum(weights, axis=1, keepdims=True), den_ref.shape[1:])


def out_part(refs, t, num, den, lay_ref, normed_ref):
    rows = step_rows(refs["hidden"], t)
    query_raw = dot(rows.astype(bf16), refs["projections"][2], 1, 0)
    summary = num / den
    _, _, _, _, attention = weigh_out(query_raw, summary)
    blended = rounded_dot(attention, summary, 0, 0)
    normed = (blended * inverse_norm(blended)).astype(bf16)
    layer = (rows + dot(normed, refs["w_out"], 1, 0)).astype(bf16).astype(f32)
    lay_ref[:, t] = layer.reshape(lay_ref.shape[0], *lay_ref.shape[2:])


def out_back_part(refs, t, num, den, ds_ref, dq_ref, go_ref):
    hidden = step_rows(refs["hidden"], t).astype(bf16)
    query_raw = dot(hidden, refs["projections"][2], 1, 0)
    cotangent = step_rows(refs["cotangent"], t).astype(bf16)
    summary = num / den
    inverse, unit, pooled_inverse, pooled, attention = weigh_out(query_raw, summary)
    scale = scale_of(query_raw.shape[-1])
    blended = rounded_dot(attention, summary, 0, 0)
    blended_inverse = inverse_norm(blended)
    normed = blended * blended_inverse
    go_ref[...] += dot(normed.astype(bf16), cotangent, 0, 0)
    d_normed = dot(cotangent, refs["w_out"], 1, 1).astype(bf16).astype(f32)
    d_blended = normalize_back(blended_inverse, normed, d_normed)
    d_attention = rounded_dot(summary, d_blended, 1, 1)
    d_scores = attention * (
        d_attention - jnp.sum(attention * d_attention, axis=0, keepdims=True)
    )
    d_unit = scale * rounded_dot(d_scores, pooled, 0, 0)
    d_pooled = scale * rounded_dot(d_scores, unit, 1, 0)
    ds_ref[t] = rounded_dot(attention, d_blended, 1, 0) + normalize_back(
        pooled_inverse, pooled, d_pooled
    )
    dq_ref[t] = normalize_back(inverse, unit, d_unit).astype(bf16)


def in_back_part(refs, t, num, den, d_summary, d_query, dh_ref, grads):
    hidden, key_raw, values, _ = project(refs["hidden"], t, *refs["projections"])
    cotangent = step_rows(refs["cotangent"], t)
    projector = refs["projector"]
    inverse, unit, weights = weigh_in(key_raw, projector)
    scale = scale_of(key_raw.shape[-1])
    d_num = d_summary / den
    d_den = -jnp.sum(d_summary * num, axis=1, keepdims=True) / (den * den)[:, :1]
    d_weights = rounded_dot(d_num, values, 1, 1) + d_den
    d_scores = d_weights * weights
    mapping_inverse = inverse_norm(projector)
    mapping = projector * mapping_inverse
    d_unit = scale * rounded_dot(d_scores, mapping, 0, 0)
    d_mapping = scale * rounded_dot(d_scores, unit, 1, 0)
    d_key = normalize_back(inverse, unit, d_unit).astype(bf16)
    d_values = rounded_dot(weights, d_num, 0, 0).astype(bf16)
    w_key, w_value, w_query = refs["projections"]
    together = jnp.concatenate([d_key, d_values, d_query], axis=1)
    turned = jnp.concatenate([w_key, w_value, w_query], axis=1)
    d_hidden = cotangent + dot(together, turned, 1, 1)
    dh_ref[:, t] = d_hidden.reshape(dh_ref.shape[0], *dh_ref.shape[2:])
    width = w_key.shape[1]
    gradients = dot(hidden, together, 0, 0)
    for i, grad in enumerate(grads[1:]):
        grad[...] += gradients[:, i * width : (i + 1) * width]
    grads[0][...] += normalize_back(mapping_inverse, mapping, d_mapping)


def read_refs(hidden, projector, wk, wv, wq, wo=None, cotangent=None):
    return {
        "hidden": hidden,
        "projector": projector[...],
        "projections": (wk[...], wv[...], wq[...]),
        "w_out": None if wo is None else wo[...],
        "cotangent": cotangent,
    }


def in_kernel(hidden, projector, wk, wv, wq, num_ref, den_ref):
    refs = read_refs(hidden, projector, wk, wv, wq)
    for t in range(hidden.shape[1]):
        in_part(refs, t, num_ref, den_ref)


def out_kernel(hidden, projector, wk, wv, wq, wo, num_ref, den_ref, lay_ref):
    refs = read_refs(hidden, projector, wk, wv, wq, wo)
    for t in range(hidden.shape[1]):
        out_part(refs, t, num_ref[t], den_ref[t], lay_ref, None)


def forward_kernel(hidden, projector, wk, wv, wq, wo, num_ref, den_ref, lay_ref):
    in_kernel(hidden, projector, wk, wv, wq, num_ref, den_ref)
    out_kernel(hidden, projector, wk, wv, wq, wo, num_ref, den_ref, lay_ref)


def out_back_kernel(hidden, projector, wk, wv, wq, wo, cot, num_ref, den_ref, ds_ref, dq_ref, go_ref):
    refs = read_refs(hidden, projector, wk, wv, wq, wo, cot)
    go_ref[...] = jnp.zeros_like(go_ref)
    for t in range(hidden.shape[1]):
        out_back_part(refs, t, num_ref[t], den_ref[t], ds_ref, dq_ref, go_ref)


def lay_partials(part_ref, grads):
    owners = part_ref.shape[0]
    for m in range(owners):
        at = 0
        for grad in grads:
            own = grad.shape[0] // owners
            part_ref[m, at : at + own, :] = grad[m * own : (m + 1) * own, :]
            at += own
        if at < part_ref.shape[1]:
            part_ref[m, at:, :] = jnp.zeros((part_ref.shape[1] - at, part_ref.shape[2]), f32)


def in_back_kernel(
    hidden, projector, wk, wv, wq, wo, cot, num_ref, den_ref, ds_ref, dq_ref, go_ref,
    dh_ref, part_ref, gp, gk, gv, gq,
):
    refs = read_refs(hidden, projector, wk, wv, wq, wo, cot)
    grads = (gp, gk, gv, gq)
    for grad in grads:
        grad[...] = jnp.zeros_like(grad)
    for t in range(hidden.shape[1]):
        in_back_part(refs, t, num_ref[t], den_ref[t], ds_ref[t], dq_ref[t], dh_ref, grads)
    lay_partials(part_ref, grads + (go_ref,))


def backward_kernel(
    hidden, projector, wk, wv, wq, wo, cot, num_ref, den_ref,
    dh_ref, part_ref, gp, gk, gv, gq, ds_ref, dq_ref, go_ref,
):
    out_back_kernel(
        hidden, projector, wk, wv, wq, wo, cot, num_ref, den_ref, ds_ref, dq_ref, go_ref
    )
    in_back_kernel(
        hidden, projector, wk, wv, wq, wo, cot, num_ref, den_ref, ds_ref, dq_ref, go_ref,
        dh_ref, part_ref, gp, gk, gv, gq,
    )


def fold_kernel(parts_ref, out_ref):
    total = parts_ref[0]
    for i in range(1, parts_ref.shape[0]):
        total = total + parts_ref[i]
    out_ref[...] = total


def fold(parts):
    return pl.pallas_call(
        fold_kernel,
        out_shape=jax.ShapeDtypeStruct(parts.shape[1:], f32),
        compiler_params=params(),
    )(parts)


def deal_kernel(rows_ref, *out_refs):
    at = 0
    for out in out_refs:
        out[...] = rows_ref[at : at + out.shape[0], :]
        at += out.shape[0]


def per_device(n_sensor, n_tm, inputs, mask, projector, w_key, w_value, w_query, w_out, cotangent):
    sensors, steps, width = inputs.shape
    tokens = projector.shape[0]
    group = math.gcd(n_sensor, steps)
    rest = n_sensor // group
    share = steps // group
    if rest == 1:
        swap = functools.partial(
            lax.all_to_all, axis_name="sensor", split_axis=0, concat_axis=0, tiled=True
        )
    else:
        blocks = [list(range(r * group, (r + 1) * group)) for r in range(rest)]
        swap = functools.partial(
            lax.all_to_all, axis_name="sensor", split_axis=0, concat_axis=0, tiled=True,
            axis_index_groups=blocks,
        )
        across = [list(range(i, n_sensor, group)) for i in range(group)]
    timed = (group, share, sensors, width)
    hidden = swap(outward(inputs, mask)).reshape(timed)
    cot = swap(outward(cotangent, None)).reshape(timed)
    weights = (projector, w_key, w_value, w_query)
    small = jax.ShapeDtypeStruct((share, tokens, width), f32)
    large = jax.ShapeDtypeStruct(timed, f32)
    square = jax.ShapeDtypeStruct((width, width), f32)
    query_shape = jax.ShapeDtypeStruct((share, group * sensors, width), bf16)
    owned = [tokens // n_tm] + [width // n_tm] * 4
    chunk = -(-sum(owned) // n_sensor)
    part_shape = jax.ShapeDtypeStruct((n_tm, chunk * n_sensor, width), f32)
    grad_scratch = [pltpu.VMEM((tokens, width), f32)] + [pltpu.VMEM((width, width), f32)] * 3
    if rest == 1:
        num, den, layer = pl.pallas_call(
            forward_kernel, out_shape=(small, small, large), compiler_params=params()
        )(hidden, *weights, w_out)
    else:
        num, den = pl.pallas_call(in_kernel, out_shape=(small, small), compiler_params=params())(
            hidden, *weights
        )
        num, den = lax.psum((num, den), "sensor", axis_index_groups=across)
        layer = pl.pallas_call(out_kernel, out_shape=large, compiler_params=params())(
            hidden, *weights, w_out, num, den
        )
    layer_home = swap(layer.reshape(steps, sensors, width))
    if rest == 1:
        d_hidden, part = pl.pallas_call(
            backward_kernel,
            out_shape=(large, part_shape),
            scratch_shapes=grad_scratch
            + [
                pltpu.VMEM(small.shape, f32),
                pltpu.VMEM(query_shape.shape, bf16),
                pltpu.VMEM((width, width), f32),
            ],
            compiler_params=params(),
        )(hidden, *weights, w_out, cot, num, den)
    else:
        d_summary, d_query, grad_out = pl.pallas_call(
            out_back_kernel, out_shape=(small, query_shape, square), compiler_params=params()
        )(hidden, *weights, w_out, cot, num, den)
        d_summary = lax.psum(d_summary, "sensor", axis_index_groups=across)
        d_hidden, part = pl.pallas_call(
            in_back_kernel,
            out_shape=(large, part_shape),
            scratch_shapes=grad_scratch,
            compiler_params=params(),
        )(hidden, *weights, w_out, cot, num, den, d_summary, d_query, grad_out)
    me = lax.axis_index("tm")
    terms = [lax.dynamic_index_in_dim(part, me, 0, keepdims=False)]
    for step in range(1, n_tm):
        gone = lax.dynamic_index_in_dim(part, lax.rem(me + step, n_tm), 0, keepdims=False)
        ring = [(i, (i + step) % n_tm) for i in range(n_tm)]
        terms.append(lax.ppermute(gone, "tm", ring))
    mine = sum(terms[1:], terms[0]).reshape(n_sensor, chunk, width)
    whole_swap = functools.partial(
        lax.all_to_all, axis_name="sensor", split_axis=0, concat_axis=0, tiled=True
    )
    total = fold(whole_swap(mine))
    gathered = whole_swap(jnp.broadcast_to(total[None], (n_sensor, chunk, width)))
    d_home = swap(d_hidden.reshape(steps, sensors, width))
    output_rows = homeward(layer_home, None)
    d_inputs = homeward(d_home, mask)
    outs = pl.pallas_call(
        deal_kernel,
        out_shape=tuple(jax.ShapeDtypeStruct((n, width), f32) for n in owned),
        compiler_params=params(),
    )(gathered.reshape(n_sensor * chunk, width))
    return (output_rows, d_inputs, *outs)


def solution(mesh):
    placed = (
        P("sensor", "tm", None),
        P("sensor", "tm"),
        P(),
        P(),
        P(),
        P(),
        P(),
        P("sensor", "tm", None),
    )
    return jax.shard_map(
        functools.partial(per_device, mesh.shape["sensor"], mesh.shape["tm"]),
        mesh=mesh,
        in_specs=placed,
        out_specs=(
            P("sensor", "tm", None),
            P("sensor", "tm", None),
            P("tm", None),
            P("tm", None),
            P("tm", None),
            P("tm", None),
            P("tm", None),
        ),
        check_vma=False,
    )
```

```python
import functools
import math

import jax
import jax.numpy as jnp
from jax import lax
from jax.experimental import pallas as pl
from jax.experimental.pallas import tpu as pltpu
from jax.sharding import PartitionSpec as P

sharpness_divisor = 12.0
epsilon = 1e-06
f32 = jnp.float32
bf16 = jnp.bfloat16


def params():
    return pltpu.CompilerParams(vmem_limit_bytes=48 * 1024 * 1024)


def dot(left, right, left_dim, right_dim):
    return lax.dot_general(
        left, right, (((left_dim,), (right_dim,)), ((), ())), preferred_element_type=f32
    )


def rounded_dot(left, right, left_dim, right_dim):
    return dot(left.astype(bf16), right.astype(bf16), left_dim, right_dim)


def inverse_norm(vector):
    return lax.rsqrt(jnp.mean(vector * vector, axis=-1, keepdims=True) + epsilon)


def normalize_back(inverse, unit, gradient):
    return inverse * (gradient - unit * jnp.mean(unit * gradient, axis=-1, keepdims=True))


def outward_kernel(inputs_ref, mask_ref, cotangent_ref, out_ref, wide, wide_cotangent):
    sensors, steps, _ = inputs_ref.shape
    share = steps // out_ref.shape[0]
    wide[...] = inputs_ref[...].astype(f32)
    wide_cotangent[...] = cotangent_ref[...].astype(f32)
    marks = mask_ref[...].astype(f32)
    for t in range(steps):
        place, own = divmod(t, share)
        out_ref[place, own * sensors : (own + 1) * sensors, :] = (
            wide[:, t, :] * marks[:, t : t + 1]
        )
        at = (share + own) * sensors
        out_ref[place, at : at + sensors, :] = wide_cotangent[:, t, :]


def homeward_kernel(rows_ref, mask_ref, layer_ref, d_inputs_ref, wide, wide_gradient):
    sensors, steps, _ = layer_ref.shape
    share = steps // rows_ref.shape[0]
    marks = mask_ref[...].astype(f32)
    for t in range(steps):
        place, own = divmod(t, share)
        wide[:, t, :] = rows_ref[place, own * sensors : (own + 1) * sensors, :]
        at = (share + own) * sensors
        wide_gradient[:, t, :] = rows_ref[place, at : at + sensors, :] * marks[:, t : t + 1]
    layer_ref[...] = wide[...].astype(bf16)
    d_inputs_ref[...] = wide_gradient[...].astype(bf16)


def rows_of(ref, block, sensors):
    rows = ref[:, block * sensors : (block + 1) * sensors, :]
    return rows.reshape(rows.shape[0] * sensors, rows.shape[2])


def put_rows(ref, block, sensors, rows):
    ref[:, block * sensors : (block + 1) * sensors, :] = rows.reshape(
        ref.shape[0], sensors, rows.shape[1]
    )


def scale_of(width):
    return sharpness_divisor / width


def weigh_in(key_raw, projector):
    inverse = inverse_norm(key_raw)
    unit = key_raw * inverse
    mapping = projector * inverse_norm(projector)
    scale = scale_of(key_raw.shape[-1])
    return inverse, unit, jnp.exp(scale * rounded_dot(mapping, unit, 1, 1))


def diagonal(tokens):
    rows = lax.broadcasted_iota(jnp.int32, (tokens, tokens), 0)
    return rows == lax.broadcasted_iota(jnp.int32, (tokens, tokens), 1)


def in_kernel(share, sensors, swapped, projector, wk, wv, sums_ref):
    tokens, width = projector.shape
    same = diagonal(tokens)
    tail = share * tokens
    sums_ref[tail:, :] = jnp.zeros((sums_ref.shape[0] - tail, width), f32)
    both_weights = jnp.concatenate([wk[...], wv[...]], axis=1)
    for t in range(share):
        hidden = rows_of(swapped, t, sensors).astype(bf16)
        both = dot(hidden, both_weights, 1, 0)
        _, _, weights = weigh_in(both[:, :width], projector[...])
        sums_ref[t * tokens : (t + 1) * tokens, :] = rounded_dot(weights, both[:, width:], 1, 0)
        den = jnp.sum(weights, axis=1, keepdims=True)
        sums_ref[tail + t : tail + t + 1, :tokens] = jnp.sum(
            jnp.where(same, den, 0.0), axis=0, keepdims=True
        )


def total_of(refs):
    total = refs[0][...]
    for ref in refs[1:]:
        total = total + ref[...]
    return total


def num_den(total, t, share, tokens):
    num = total[t * tokens : (t + 1) * tokens, :]
    at = share * tokens + t
    den = jnp.sum(
        jnp.where(diagonal(tokens), total[at : at + 1, :tokens], 0.0), axis=1, keepdims=True
    )
    return num, den


def out_kernel(share, sensors, terms, swapped, wq, wo, *refs):
    sums = refs[:terms]
    lay_ref, ds_ref, dq_ref, go_ref = refs[terms:]
    width = wq.shape[0]
    tokens = ds_ref.shape[0] // share
    scale = scale_of(width)
    total = total_of(sums)
    w_out = wo[...]
    for t in range(share):
        rows = rows_of(swapped, t, sensors)
        query_raw = dot(rows.astype(bf16), wq[...], 1, 0)
        cotangent = rows_of(swapped, share + t, sensors).astype(bf16)
        num, den = num_den(total, t, share, tokens)
        summary = num / den
        inverse = inverse_norm(query_raw)
        unit = query_raw * inverse
        pooled_inverse = inverse_norm(summary)
        pooled = summary * pooled_inverse
        weights = jnp.exp(scale * rounded_dot(pooled, unit, 1, 1))
        attention = weights / jnp.sum(weights, axis=0, keepdims=True)
        blended = rounded_dot(attention, summary, 0, 0)
        blended_inverse = inverse_norm(blended)
        normed = blended * blended_inverse
        rounded = normed.astype(bf16)
        layer = (rows + dot(rounded, w_out, 1, 0)).astype(bf16).astype(f32)
        put_rows(lay_ref, t, sensors, layer)
        grad_out = dot(rounded, cotangent, 0, 0)
        go_ref[...] = grad_out if t == 0 else go_ref[...] + grad_out
        d_normed = dot(cotangent, w_out, 1, 1).astype(bf16).astype(f32)
        d_blended = normalize_back(blended_inverse, normed, d_normed)
        d_attention = rounded_dot(summary, d_blended, 1, 1)
        d_scores = attention * (
            d_attention - jnp.sum(attention * d_attention, axis=0, keepdims=True)
        )
        d_unit = scale * rounded_dot(d_scores, pooled, 0, 0)
        d_pooled = scale * rounded_dot(d_scores, unit, 1, 0)
        ds_ref[t * tokens : (t + 1) * tokens, :] = rounded_dot(
            attention, d_blended, 1, 0
        ) + normalize_back(pooled_inverse, pooled, d_pooled)
        d_query = normalize_back(inverse, unit, d_unit).astype(bf16)
        dq_ref[t * d_query.shape[0] : (t + 1) * d_query.shape[0], :] = d_query


def put_partials(ref, base, owners, chunk, grads):
    for m in range(owners):
        at = 0
        for grad in grads:
            own = grad.shape[0] // owners
            done = 0
            while done < own:
                place, row = divmod(at, chunk)
                count = min(own - done, chunk - row)
                begin = base + m * chunk + row
                start = m * own + done
                ref[place, begin : begin + count, :] = grad[start : start + count, :]
                done += count
                at += count
        while at < ref.shape[0] * chunk:
            place, row = divmod(at, chunk)
            begin = base + m * chunk + row
            ref[place, begin : begin + chunk - row, :] = jnp.zeros((chunk - row, ref.shape[2]), f32)
            at += chunk - row


def in_back_kernel(share, sensors, terms, owners, chunk, swapped, projector, wk, wv, wq, lay_ref, dq_ref, go_ref, *refs):
    sums, d_sums = refs[:terms], refs[terms : 2 * terms]
    out_ref = refs[2 * terms]
    tokens, width = projector.shape
    scale = scale_of(width)
    total = total_of(sums)
    d_total = total_of(d_sums)
    mapping_inverse = inverse_norm(projector[...])
    mapping = projector[...] * mapping_inverse
    w_key, w_value, w_query = wk[...], wv[...], wq[...]
    both_weights = jnp.concatenate([w_key, w_value], axis=1)
    turned = jnp.concatenate([w_key, w_value, w_query], axis=1)
    out_ref[:, : share * sensors, :] = lay_ref[...]
    gradients = None
    for t in range(share):
        hidden = rows_of(swapped, t, sensors).astype(bf16)
        both = dot(hidden, both_weights, 1, 0)
        values = both[:, width:].astype(bf16)
        cotangent = rows_of(swapped, share + t, sensors)
        inverse, unit, weights = weigh_in(both[:, :width], projector[...])
        num, den = num_den(total, t, share, tokens)
        d_summary = d_total[t * tokens : (t + 1) * tokens, :]
        d_num = d_summary / den
        d_den = -jnp.sum(d_summary * num, axis=1, keepdims=True) / (den * den)
        d_scores = (rounded_dot(d_num, values, 1, 1) + d_den) * weights
        d_unit = scale * rounded_dot(d_scores, mapping, 0, 0)
        d_mapping = scale * rounded_dot(d_scores, unit, 1, 0)
        d_key = normalize_back(inverse, unit, d_unit).astype(bf16)
        d_values = rounded_dot(weights, d_num, 0, 0).astype(bf16)
        d_query = dq_ref[t * hidden.shape[0] : (t + 1) * hidden.shape[0], :]
        together = jnp.concatenate([d_key, d_values, d_query], axis=1)
        put_rows(out_ref, share + t, sensors, cotangent + dot(together, turned, 1, 1))
        more = (normalize_back(mapping_inverse, mapping, d_mapping), dot(hidden, together, 0, 0))
        gradients = more if t == 0 else tuple(a + b for a, b in zip(gradients, more))
    parts = [gradients[0]] + [gradients[1][:, i * width : (i + 1) * width] for i in range(3)]
    put_partials(out_ref, 2 * share * sensors, owners, chunk, parts + [go_ref[...]])


def fold_kernel(base, parts_ref, out_ref):
    total = parts_ref[0, base:, :]
    for i in range(1, parts_ref.shape[0]):
        total = total + parts_ref[i, base:, :]
    out_ref[...] = total.reshape(out_ref.shape)


def deal_kernel(rows_ref, *out_refs):
    at = 0
    for out in out_refs:
        out[...] = rows_ref[at : at + out.shape[0], :]
        at += out.shape[0]


def call(kernel, out_shape, *args, **more):
    return pl.pallas_call(kernel, out_shape=out_shape, compiler_params=params(), **more)(*args)


def group_size(n_sensor, steps):
    group = math.gcd(n_sensor, steps)
    return group // 2 if group % 2 == 0 and group > 8 else group


def per_device(n_sensor, n_tm, inputs, mask, projector, w_key, w_value, w_query, w_out, cotangent):
    sensors, steps, width = inputs.shape
    tokens = projector.shape[0]
    group = group_size(n_sensor, steps)
    rest = n_sensor // group
    share = steps // group
    blocks = [list(range(r * group, (r + 1) * group)) for r in range(rest)]

    def swap(rows):
        return lax.all_to_all(rows, "sensor", 0, 0, tiled=True, axis_index_groups=blocks)

    def others(rows):
        return [
            lax.ppermute(
                rows, "sensor", [(i, (i + step * group) % n_sensor) for i in range(n_sensor)]
            )
            for step in range(1, rest)
        ]

    def shape(*dims, kind=f32):
        return jax.ShapeDtypeStruct(dims, kind)

    wide = pltpu.VMEM(inputs.shape, f32)
    swapped = swap(
        call(
            outward_kernel,
            shape(group, 2 * share * sensors, width),
            inputs, mask, cotangent,
            scratch_shapes=[wide, wide],
        )
    )
    n_rows = group * sensors
    sums_rows = share * tokens + -(-share // 8) * 8
    sums = call(
        functools.partial(in_kernel, share, sensors),
        shape(sums_rows, width),
        swapped, projector, w_key, w_value,
    )
    sums = [sums] + others(sums)
    layer, d_sums, d_query, grad_out = call(
        functools.partial(out_kernel, share, sensors, rest),
        (
            shape(group, share * sensors, width),
            shape(share * tokens, width),
            shape(share * n_rows, width, kind=bf16),
            shape(width, width),
        ),
        swapped, w_query, w_out, *sums,
    )
    d_sums = [d_sums] + others(d_sums)
    owned = [tokens // n_tm] + [width // n_tm] * 4
    chunk = -(-sum(owned) // (8 * group)) * 8
    base = 2 * share * sensors
    back = call(
        functools.partial(in_back_kernel, share, sensors, rest, n_tm, chunk),
        shape(group, base + n_tm * chunk, width),
        swapped, projector, w_key, w_value, w_query, layer, d_query, grad_out, *sums, *d_sums,
    )
    home = swap(back)
    part = call(functools.partial(fold_kernel, base), shape(n_tm, chunk, width), home)
    me = lax.axis_index("tm")
    mine = lax.dynamic_index_in_dim(part, me, 0, keepdims=False)
    for step in range(1, n_tm):
        gone = lax.dynamic_index_in_dim(part, lax.rem(me + step, n_tm), 0, keepdims=False)
        ring = [(i, (i + step) % n_tm) for i in range(n_tm)]
        mine = mine + lax.ppermute(gone, "tm", ring)
    mine = sum(others(mine), mine)
    gathered = swap(jnp.broadcast_to(mine[None], (group, chunk, width)))
    output_rows, d_inputs = call(
        homeward_kernel,
        (shape(*inputs.shape, kind=bf16), shape(*inputs.shape, kind=bf16)),
        home, mask,
        scratch_shapes=[wide, wide],
    )
    outs = call(
        deal_kernel,
        tuple(shape(n, width) for n in owned),
        gathered.reshape(group * chunk, width),
    )
    return (output_rows, d_inputs, *outs)


def solution(mesh):
    placed = (
        P("sensor", "tm", None),
        P("sensor", "tm"),
        P(),
        P(),
        P(),
        P(),
        P(),
        P("sensor", "tm", None),
    )
    return jax.shard_map(
        functools.partial(per_device, mesh.shape["sensor"], mesh.shape["tm"]),
        mesh=mesh,
        in_specs=placed,
        out_specs=(
            P("sensor", "tm", None),
            P("sensor", "tm", None),
            P("tm", None),
            P("tm", None),
            P("tm", None),
            P("tm", None),
            P("tm", None),
        ),
        check_vma=False,
    )
```

```python
import functools

import jax
import jax.numpy as jnp
from jax import lax
from jax.experimental import pallas as pl
from jax.experimental.pallas import tpu as pltpu
from jax.sharding import PartitionSpec as P

sharpness_divisor = 12.0
epsilon = 1e-06
f32 = jnp.float32
bf16 = jnp.bfloat16


def params(mebibytes=32):
    return pltpu.CompilerParams(vmem_limit_bytes=mebibytes * 1024 * 1024)


def dot(left, right, left_dim, right_dim):
    return lax.dot_general(
        left, right, (((left_dim,), (right_dim,)), ((), ())), preferred_element_type=f32
    )


def rounded_dot(left, right, left_dim, right_dim):
    return dot(left.astype(bf16), right.astype(bf16), left_dim, right_dim)


def inverse_norm(vector):
    return lax.rsqrt(jnp.mean(vector * vector, axis=-1, keepdims=True) + epsilon)


def normalize_back(inverse, unit, gradient):
    return inverse * (gradient - unit * jnp.mean(unit * gradient, axis=-1, keepdims=True))


def diagonal(tokens):
    rows = lax.broadcasted_iota(jnp.int32, (tokens, tokens), 0)
    return rows == lax.broadcasted_iota(jnp.int32, (tokens, tokens), 1)


def turned_mask(mask_ref):
    sensors = mask_ref.shape[1]
    return dot(diagonal(sensors).astype(f32).astype(bf16), mask_ref[...].astype(f32).astype(bf16), 1, 1)


def outward_kernel(inputs_ref, mask_ref, cotangent_ref, far_ref, near, near_cotangent, wide, out_ref, sems):
    sensors, steps, _ = inputs_ref.shape
    places = out_ref.shape[0]
    share = steps // places
    rows = share * sensors
    first = pltpu.make_async_copy(inputs_ref, near, sems.at[2 * places])
    second = pltpu.make_async_copy(cotangent_ref, near_cotangent, sems.at[2 * places + 1])
    first.start()
    second.start()
    marks = turned_mask(mask_ref)
    sent = []

    def send(place, half):
        block = (place, pl.ds(half * rows, rows))
        copy = pltpu.make_async_copy(
            out_ref.at[block], far_ref.at[block], sems.at[half * places + place]
        )
        copy.start()
        sent.append(copy)

    first.wait()
    wide[...] = near[...].astype(f32)
    for place in range(places):
        for own in range(share):
            t = place * share + own
            out_ref[place, own * sensors : (own + 1) * sensors, :] = (
                wide[:, t, :] * marks[:, t : t + 1]
            )
        send(place, 0)
    second.wait()
    wide[...] = near_cotangent[...].astype(f32)
    for place in range(places):
        for own in range(share):
            at = rows + own * sensors
            out_ref[place, at : at + sensors, :] = wide[:, place * share + own, :]
        send(place, 1)
    for copy in sent:
        copy.wait()


def homeward_kernel(rows_ref, mask_ref, layer_ref, d_inputs_ref, wide, wide_gradient):
    sensors, steps, _ = layer_ref.shape
    share = steps // rows_ref.shape[0]
    marks = turned_mask(mask_ref)
    for t in range(steps):
        place, own = divmod(t, share)
        wide[:, t, :] = rows_ref[place, own * sensors : (own + 1) * sensors, :]
        at = (share + own) * sensors
        wide_gradient[:, t, :] = rows_ref[place, at : at + sensors, :] * marks[:, t : t + 1]
    layer_ref[...] = wide[...].astype(bf16)
    d_inputs_ref[...] = wide_gradient[...].astype(bf16)


def rows_of(ref, block, sensors):
    rows = ref[:, block * sensors : (block + 1) * sensors, :]
    return rows.reshape(rows.shape[0] * sensors, rows.shape[2])


def put_rows(ref, block, sensors, rows):
    ref[:, block * sensors : (block + 1) * sensors, :] = rows.reshape(
        ref.shape[0], sensors, rows.shape[1]
    )


def scale_of(width):
    return sharpness_divisor / width


def weigh_in(key_raw, projector):
    inverse = inverse_norm(key_raw)
    unit = key_raw * inverse
    mapping = projector * inverse_norm(projector)
    scale = scale_of(key_raw.shape[-1])
    return inverse, unit, jnp.exp(scale * rounded_dot(mapping, unit, 1, 1))


def in_kernel(share, sensors, swapped, projector, wk, wv, sums_ref):
    tokens, width = projector.shape
    same = diagonal(tokens)
    tail = share * tokens
    sums_ref[tail:, :] = jnp.zeros((sums_ref.shape[0] - tail, width), f32)
    both_weights = jnp.concatenate([wk[...], wv[...]], axis=1)
    for t in range(share):
        hidden = rows_of(swapped, t, sensors).astype(bf16)
        both = dot(hidden, both_weights, 1, 0)
        _, _, weights = weigh_in(both[:, :width], projector[...])
        sums_ref[t * tokens : (t + 1) * tokens, :] = rounded_dot(weights, both[:, width:], 1, 0)
        den = jnp.sum(weights, axis=1, keepdims=True)
        sums_ref[tail + t : tail + t + 1, :tokens] = jnp.sum(
            jnp.where(same, den, 0.0), axis=0, keepdims=True
        )


def total_of(refs):
    total = refs[0][...]
    for ref in refs[1:]:
        total = total + ref[...]
    return total


def num_den(total, t, share, tokens):
    num = total[t * tokens : (t + 1) * tokens, :]
    at = share * tokens + t
    den = jnp.sum(
        jnp.where(diagonal(tokens), total[at : at + 1, :tokens], 0.0), axis=1, keepdims=True
    )
    return num, den


def ready_kernel(
    share, sensors, swapped, projector, wk, wv, wq, wo,
    in_ref, out_ref,
):
    width = wk.shape[0]
    tokens = projector.shape[0]
    together = jnp.concatenate([wk[...], wv[...], wq[...]], axis=1)
    for t in range(share):
        hidden = rows_of(swapped, t, sensors).astype(bf16)
        at = slice(t * hidden.shape[0], (t + 1) * hidden.shape[0])
        raw = dot(hidden, together, 1, 0)
        inverse, unit, weights = weigh_in(raw[:, :width], projector[...])
        query_raw = raw[:, 2 * width :]
        query_inverse = inverse_norm(query_raw)
        in_ref[0, at, :] = unit
        in_ref[1, at, :] = jnp.broadcast_to(inverse, unit.shape)
        in_ref[2, at, :] = raw[:, width : 2 * width].astype(bf16).astype(f32)
        for block in range(hidden.shape[0] // width):
            to = block * tokens + t * hidden.shape[0]
            in_ref[3, to : to + tokens, :] = weights[:, block * width : (block + 1) * width]
        out_ref[0, at, :] = query_raw * query_inverse
        out_ref[1, at, :] = jnp.broadcast_to(query_inverse, unit.shape)
        cotangent = rows_of(swapped, share + t, sensors).astype(bf16)
        out_ref[2, at, :] = dot(cotangent, wo[...], 1, 1).astype(bf16).astype(f32)


def out_kernel(share, terms, ready_ref, *refs):
    sums, (ds_ref, normed_ref, d_scores_ref) = refs[:terms], refs[terms:]
    width = ready_ref.shape[2]
    tokens = ds_ref.shape[0] // share
    scale = scale_of(width)
    total = total_of(sums)
    n_rows = ready_ref.shape[1] // share
    for t in range(share):
        at = slice(t * n_rows, (t + 1) * n_rows)
        own = slice(t * tokens, (t + 1) * tokens)
        unit = ready_ref[0, at, :]
        num, den = num_den(total, t, share, tokens)
        summary = num / den
        pooled_inverse = inverse_norm(summary)
        pooled = summary * pooled_inverse
        weights = jnp.exp(scale * rounded_dot(pooled, unit, 1, 1))
        attention = weights / jnp.sum(weights, axis=0, keepdims=True)
        blended = rounded_dot(attention, summary, 0, 0)
        blended_inverse = inverse_norm(blended)
        normed = blended * blended_inverse
        normed_ref[at, :] = normed.astype(bf16)
        d_blended = normalize_back(blended_inverse, normed, ready_ref[2, at, :])
        d_attention = rounded_dot(summary, d_blended, 1, 1)
        d_scores = attention * (
            d_attention - jnp.sum(attention * d_attention, axis=0, keepdims=True)
        )
        d_pooled = scale * rounded_dot(d_scores, unit, 1, 0)
        ds_ref[own, :] = rounded_dot(attention, d_blended, 1, 0) + normalize_back(
            pooled_inverse, pooled, d_pooled
        )
        d_scores_ref[own, :] = d_scores


def query_kernel(share, sensors, terms, swapped, wq, wo, ready_ref, normed_ref, d_scores_ref, *refs):
    sums, (lay_ref, dh_ref) = refs[:terms], refs[terms:]
    width = wq.shape[0]
    tokens = d_scores_ref.shape[0] // share
    scale = scale_of(width)
    total = total_of(sums)
    n_rows = ready_ref.shape[1] // share
    grad_rows = share * n_rows
    for t in range(share):
        at = slice(t * n_rows, (t + 1) * n_rows)
        rows = rows_of(swapped, t, sensors)
        cotangent = rows_of(swapped, share + t, sensors)
        normed = normed_ref[at, :]
        layer = (rows + dot(normed, wo[...], 1, 0)).astype(bf16).astype(f32)
        put_rows(lay_ref, t, sensors, layer)
        grad_out = dot(normed, cotangent.astype(bf16), 0, 0)
        num, den = num_den(total, t, share, tokens)
        summary = num / den
        pooled = summary * inverse_norm(summary)
        d_unit = scale * rounded_dot(d_scores_ref[t * tokens : (t + 1) * tokens, :], pooled, 0, 0)
        d_query = normalize_back(ready_ref[1, at, :], ready_ref[0, at, :], d_unit).astype(bf16)
        grad_query = dot(rows.astype(bf16), d_query, 0, 0)
        dh_ref[at, :] = cotangent + dot(d_query, wq[...], 1, 1)
        for i, grad in enumerate((grad_query, grad_out)):
            to = slice(grad_rows + i * width, grad_rows + (i + 1) * width)
            dh_ref[to, :] = grad if t == 0 else dh_ref[to, :] + grad


def put_partials(ref, grads):
    owners, rows, width = ref.shape
    for m in range(owners):
        at = 0
        for grad in grads:
            own = grad.shape[0] // owners
            ref[m, at : at + own, :] = grad[m * own : (m + 1) * own, :]
            at += own
        if at < rows:
            ref[m, at:, :] = jnp.zeros((rows - at, width), f32)


def in_back_kernel(
    share, sensors, terms, swapped, projector, wk, wv, ready_ref, dh_ref, layer_ref, *refs
):
    sums, d_sums = refs[:terms], refs[terms : 2 * terms]
    out_ref, part_ref = refs[2 * terms :]
    out_ref[:, : share * sensors, :] = layer_ref[...]
    tokens, width = projector.shape
    scale = scale_of(width)
    total = total_of(sums)
    d_total = total_of(d_sums)
    mapping_inverse = inverse_norm(projector[...])
    mapping = projector[...] * mapping_inverse
    turned = jnp.concatenate([wk[...], wv[...]], axis=1)
    gradients = None
    n_rows = ready_ref.shape[1] // share
    grad_rows = share * n_rows
    for t in range(share):
        at = slice(t * n_rows, (t + 1) * n_rows)
        own = slice(t * tokens, (t + 1) * tokens)
        hidden = rows_of(swapped, t, sensors).astype(bf16)
        unit = ready_ref[0, at, :]
        weights = jnp.concatenate(
            [
                ready_ref[3, t * n_rows + i * tokens : t * n_rows + (i + 1) * tokens, :]
                for i in range(n_rows // width)
            ],
            axis=1,
        )
        num, den = num_den(total, t, share, tokens)
        d_summary = d_total[own, :]
        d_num = d_summary / den
        d_den = -jnp.sum(d_summary * num, axis=1, keepdims=True) / (den * den)
        d_scores = (rounded_dot(d_num, ready_ref[2, at, :], 1, 1) + d_den) * weights
        d_unit = scale * rounded_dot(d_scores, mapping, 0, 0)
        d_mapping = scale * rounded_dot(d_scores, unit, 1, 0)
        d_key = normalize_back(ready_ref[1, at, :], unit, d_unit).astype(bf16)
        d_values = rounded_dot(weights, d_num, 0, 0).astype(bf16)
        together = jnp.concatenate([d_key, d_values], axis=1)
        d_hidden = dh_ref[at, :] + dot(together, turned, 1, 1)
        put_rows(out_ref, share + t, sensors, d_hidden)
        more = (normalize_back(mapping_inverse, mapping, d_mapping), dot(hidden, together, 0, 0))
        gradients = more if t == 0 else tuple(a + b for a, b in zip(gradients, more))
    parts = [gradients[0], gradients[1][:, :width], gradients[1][:, width:]]
    parts += [dh_ref[grad_rows + i * width : grad_rows + (i + 1) * width, :] for i in range(2)]
    put_partials(part_ref, parts)


def deal_kernel(count, place_ref, *refs):
    chunks, out_refs, rows = refs[:count], refs[count:-1], refs[-1]
    for m, chunk in enumerate(chunks):
        source = lax.bitwise_xor(place_ref[0], m)
        rows[pl.ds(source * chunk.shape[0], chunk.shape[0]), :] = chunk[...]
    at = 0
    for out in out_refs:
        out[...] = rows[at : at + out.shape[0], :]
        at += out.shape[0]


def call(kernel, out_shape, *args, vmem=32, **more):
    return pl.pallas_call(kernel, out_shape=out_shape, compiler_params=params(vmem), **more)(*args)


def group_size(most, *sizes):
    group = 1
    while group < most and all(size % (2 * group) == 0 for size in sizes):
        group *= 2
    return group


def per_device(n_sensor, n_tm, inputs, mask, projector, w_key, w_value, w_query, w_out, cotangent):
    sensors, steps, width = inputs.shape
    tokens = projector.shape[0]
    group = group_size(8, n_sensor, steps)
    rest = n_sensor // group
    share = steps // group
    blocks = [list(range(r * group, (r + 1) * group)) for r in range(rest)]

    def swap(rows):
        return lax.all_to_all(rows, "sensor", 0, 0, tiled=True, axis_index_groups=blocks)

    def others(rows):
        return [
            lax.ppermute(
                rows, "sensor", [(i, (i + step * group) % n_sensor) for i in range(n_sensor)]
            )
            for step in range(1, rest)
        ]

    def shape(*dims, kind=f32):
        return jax.ShapeDtypeStruct(dims, kind)

    wide = pltpu.VMEM(inputs.shape, f32)
    mask = mask.T

    place_spec = pl.BlockSpec(memory_space=pltpu.SMEM)
    far_spec = pl.BlockSpec(memory_space=pltpu.HBM)
    near_spec = pl.BlockSpec(memory_space=pltpu.VMEM)
    swapped = swap(
        call(
            outward_kernel,
            shape(group, 2 * share * sensors, width),
            inputs, mask, cotangent,
            vmem=60,
            in_specs=[far_spec, near_spec, far_spec],
            out_specs=far_spec,
            scratch_shapes=[
                pltpu.VMEM(inputs.shape, bf16),
                pltpu.VMEM(inputs.shape, bf16),
                wide,
                pltpu.VMEM((group, 2 * share * sensors, width), f32),
                pltpu.SemaphoreType.DMA((2 * group + 2,)),
            ],
        )
    )
    n_rows = group * sensors
    sums_rows = share * tokens + -(-share // 8) * 8
    sums = call(
        functools.partial(in_kernel, share, sensors),
        shape(sums_rows, width),
        swapped, projector, w_key, w_value,
    )
    sums = [sums] + others(sums)
    tokens_shape = shape(share * tokens, n_rows)
    owned = [tokens // n_tm] + [width // n_tm] * 4
    quarter = group_size(4, n_sensor)
    chunk = -(-sum(owned) // (8 * quarter)) * 8
    ready_in, ready_out = call(
        functools.partial(ready_kernel, share, sensors),
        (shape(4, share * n_rows, width), shape(3, share * n_rows, width)),
        swapped, projector, w_key, w_value, w_query, w_out,
    )
    d_sums, normed, d_scores = call(
        functools.partial(out_kernel, share, rest),
        (shape(share * tokens, width), shape(share * n_rows, width, kind=bf16), tokens_shape),
        ready_out, *sums,
    )
    d_sums = [d_sums] + others(d_sums)
    layer, d_hidden = call(
        functools.partial(query_kernel, share, sensors, rest),
        (
            shape(group, share * sensors, width),
            shape(share * n_rows + 2 * width, width),
        ),
        swapped, w_query, w_out, ready_out, normed, d_scores, *sums,
    )
    back, part = call(
        functools.partial(in_back_kernel, share, sensors, rest),
        (
            shape(group, 2 * share * sensors, width),
            shape(n_tm, quarter * chunk, width),
        ),
        swapped, projector, w_key, w_value, ready_in, d_hidden, layer, *sums, *d_sums,
    )
    me = lax.axis_index("tm")
    mine = lax.dynamic_index_in_dim(part, me, 0, keepdims=False)
    for step in range(1, n_tm):
        gone = lax.dynamic_index_in_dim(part, lax.rem(me + step, n_tm), 0, keepdims=False)
        ring = [(i, (i + step) % n_tm) for i in range(n_tm)]
        mine = mine + lax.ppermute(gone, "tm", ring)

    def partner(rows, m):
        return lax.ppermute(rows, "sensor", [(i, i ^ m) for i in range(n_sensor)])

    mine = mine.reshape(quarter, chunk, width)
    place = lax.rem(lax.axis_index("sensor"), quarter)
    total = lax.dynamic_index_in_dim(mine, place, 0, keepdims=False)
    for m in range(1, quarter):
        gone = lax.dynamic_index_in_dim(mine, lax.bitwise_xor(place, m), 0, keepdims=False)
        total = total + partner(gone, m)
    home = swap(back)
    output_rows, d_inputs = call(
        homeward_kernel,
        (shape(*inputs.shape, kind=bf16), shape(*inputs.shape, kind=bf16)),
        home, mask,
        scratch_shapes=[wide, wide],
    )
    m = quarter
    while n_sensor % (2 * m) == 0:
        gone = partner(total, m)
        m *= 2
        if n_sensor % (2 * m):
            total, gone, output_rows, d_inputs = lax.optimization_barrier(
                (total, gone, output_rows, d_inputs)
            )
        total = total + gone
    odd = n_sensor // m
    spread = [
        lax.ppermute(total, "sensor", [(i, (i + step * m) % n_sensor) for i in range(n_sensor)])
        for step in range(1, odd)
    ]
    total = sum(spread, total)
    chunks = [total] + [partner(total, m) for m in range(1, quarter)]
    outs = call(
        functools.partial(deal_kernel, quarter),
        tuple(shape(n, width) for n in owned),
        place[None], *chunks,
        in_specs=[place_spec] + [near_spec] * quarter,
        scratch_shapes=[pltpu.VMEM((quarter * chunk, width), f32)],
    )
    return (output_rows, d_inputs, *outs)


def solution(mesh):
    placed = (
        P("sensor", "tm", None),
        P("sensor", "tm"),
        P(),
        P(),
        P(),
        P(),
        P(),
        P("sensor", "tm", None),
    )
    return jax.shard_map(
        functools.partial(per_device, mesh.shape["sensor"], mesh.shape["tm"]),
        mesh=mesh,
        in_specs=placed,
        out_specs=(
            P("sensor", "tm", None),
            P("sensor", "tm", None),
            P("tm", None),
            P("tm", None),
            P("tm", None),
            P("tm", None),
            P("tm", None),
        ),
        check_vma=False,
    )
```

```python
import functools

import jax
import jax.numpy as jnp
from jax import lax
from jax.experimental import pallas as pl
from jax.experimental.pallas import tpu as pltpu
from jax.sharding import PartitionSpec as P

sharpness_divisor = 12.0
epsilon = 1e-06
f32 = jnp.float32
bf16 = jnp.bfloat16


def params(mebibytes=32):
    return pltpu.CompilerParams(vmem_limit_bytes=mebibytes * 1024 * 1024)


def dot(left, right, left_dim, right_dim):
    return lax.dot_general(
        left, right, (((left_dim,), (right_dim,)), ((), ())), preferred_element_type=f32
    )


def rounded_dot(left, right, left_dim, right_dim):
    return dot(left.astype(bf16), right.astype(bf16), left_dim, right_dim)


def split(value):
    high = value.astype(bf16)
    return high, (value - high.astype(f32)).astype(bf16)


def close_dot(left, right, left_dim, right_dim):
    high, low = split(left)
    right_high, right_low = split(right)
    return (
        dot(high, right_high, left_dim, right_dim)
        + dot(high, right_low, left_dim, right_dim)
        + dot(low, right_high, left_dim, right_dim)
    )


def inverse_norm(vector):
    return lax.rsqrt(jnp.mean(vector * vector, axis=-1, keepdims=True) + epsilon)


def normalize_back(inverse, unit, gradient):
    return inverse * (gradient - unit * jnp.mean(unit * gradient, axis=-1, keepdims=True))


def diagonal(tokens):
    rows = lax.broadcasted_iota(jnp.int32, (tokens, tokens), 0)
    return rows == lax.broadcasted_iota(jnp.int32, (tokens, tokens), 1)


def turned_mask(mask_ref):
    sensors = mask_ref.shape[1]
    return dot(diagonal(sensors).astype(f32).astype(bf16), mask_ref[...].astype(f32).astype(bf16), 1, 1)


def outward_kernel(inputs_ref, mask_ref, cotangent_ref, far_ref, near, near_cotangent, wide, out_ref, sems):
    sensors, steps, _ = inputs_ref.shape
    places = out_ref.shape[0]
    share = steps // places
    rows = share * sensors
    first = pltpu.make_async_copy(inputs_ref, near, sems.at[2 * places])
    second = pltpu.make_async_copy(cotangent_ref, near_cotangent, sems.at[2 * places + 1])
    first.start()
    second.start()
    marks = turned_mask(mask_ref)
    sent = []

    def send(place, half):
        block = (place, pl.ds(half * rows, rows))
        copy = pltpu.make_async_copy(
            out_ref.at[block], far_ref.at[block], sems.at[half * places + place]
        )
        copy.start()
        sent.append(copy)

    first.wait()
    wide[...] = near[...].astype(f32)
    for place in range(places):
        for own in range(share):
            t = place * share + own
            out_ref[place, own * sensors : (own + 1) * sensors, :] = (
                wide[:, t, :] * marks[:, t : t + 1]
            )
        send(place, 0)
    second.wait()
    wide[...] = near_cotangent[...].astype(f32)
    for place in range(places):
        for own in range(share):
            at = rows + own * sensors
            out_ref[place, at : at + sensors, :] = wide[:, place * share + own, :]
        send(place, 1)
    for copy in sent:
        copy.wait()


def homeward_kernel(rows_ref, mask_ref, layer_ref, d_inputs_ref, wide, wide_gradient):
    sensors, steps, _ = layer_ref.shape
    share = steps // rows_ref.shape[0]
    marks = turned_mask(mask_ref)
    for t in range(steps):
        place, own = divmod(t, share)
        wide[:, t, :] = rows_ref[place, own * sensors : (own + 1) * sensors, :]
        at = (share + own) * sensors
        wide_gradient[:, t, :] = rows_ref[place, at : at + sensors, :] * marks[:, t : t + 1]
    layer_ref[...] = wide[...].astype(bf16)
    d_inputs_ref[...] = wide_gradient[...].astype(bf16)


def rows_of(ref, block, sensors):
    rows = ref[:, block * sensors : (block + 1) * sensors, :]
    return rows.reshape(rows.shape[0] * sensors, rows.shape[2])


def put_rows(ref, block, sensors, rows):
    ref[:, block * sensors : (block + 1) * sensors, :] = rows.reshape(
        ref.shape[0], sensors, rows.shape[1]
    )


def scale_of(width):
    return sharpness_divisor / width


def weigh_in(key_raw, projector):
    inverse = inverse_norm(key_raw)
    unit = key_raw * inverse
    mapping = projector * inverse_norm(projector)
    scale = scale_of(key_raw.shape[-1])
    return inverse, unit, jnp.exp(scale * close_dot(mapping, unit, 1, 1))


def in_kernel(share, sensors, swapped, projector, wk, wv, sums_ref):
    tokens, width = projector.shape
    same = diagonal(tokens)
    tail = share * tokens
    sums_ref[tail:, :] = jnp.zeros((sums_ref.shape[0] - tail, width), f32)
    both_weights = jnp.concatenate([wk[...], wv[...]], axis=1)
    steps = range(share)
    both = [dot(rows_of(swapped, t, sensors).astype(bf16), both_weights, 1, 0) for t in steps]
    weights = [weigh_in(raw[:, :width], projector[...])[2] for raw in both]
    dens = [jnp.sum(weight, axis=1, keepdims=True) for weight in weights]
    nums = [rounded_dot(weights[t], both[t][:, width:], 1, 0) for t in steps]
    for t in steps:
        sums_ref[t * tokens : (t + 1) * tokens, :] = nums[t]
        sums_ref[tail + t : tail + t + 1, :tokens] = jnp.sum(
            jnp.where(same, dens[t], 0.0), axis=0, keepdims=True
        )


def total_of(refs):
    total = refs[0][...]
    for ref in refs[1:]:
        total = total + ref[...]
    return total


def num_den(total, t, share, tokens):
    num = total[t * tokens : (t + 1) * tokens, :]
    at = share * tokens + t
    den = jnp.sum(
        jnp.where(diagonal(tokens), total[at : at + 1, :tokens], 0.0), axis=1, keepdims=True
    )
    return num, den


def ready_kernel(
    share, sensors, swapped, projector, wk, wv, wq, wo,
    in_ref, out_ref,
):
    width = wk.shape[0]
    tokens = projector.shape[0]
    together = jnp.concatenate([wk[...], wv[...], wq[...]], axis=1)
    for t in range(share):
        hidden = rows_of(swapped, t, sensors).astype(bf16)
        at = slice(t * hidden.shape[0], (t + 1) * hidden.shape[0])
        raw = dot(hidden, together, 1, 0)
        inverse, unit, weights = weigh_in(raw[:, :width], projector[...])
        query_raw = raw[:, 2 * width :]
        query_inverse = inverse_norm(query_raw)
        in_ref[0, at, :] = unit
        in_ref[1, at, :] = jnp.broadcast_to(inverse, unit.shape)
        in_ref[2, at, :] = raw[:, width : 2 * width].astype(bf16).astype(f32)
        for block in range(hidden.shape[0] // width):
            to = block * tokens + t * hidden.shape[0]
            in_ref[3, to : to + tokens, :] = weights[:, block * width : (block + 1) * width]
        out_ref[0, at, :] = query_raw * query_inverse
        out_ref[1, at, :] = jnp.broadcast_to(query_inverse, unit.shape)
        cotangent = rows_of(swapped, share + t, sensors).astype(bf16)
        out_ref[2, at, :] = dot(cotangent, wo[...], 1, 1).astype(bf16).astype(f32)


def out_kernel(share, terms, ready_ref, *refs):
    sums, (ds_ref, normed_ref, d_scores_ref) = refs[:terms], refs[terms:]
    width = ready_ref.shape[2]
    tokens = ds_ref.shape[0] // share
    scale = scale_of(width)
    total = total_of(sums)
    n_rows = ready_ref.shape[1] // share
    steps = range(share)
    units = [ready_ref[0, t * n_rows : (t + 1) * n_rows, :] for t in steps]
    summaries = []
    for t in steps:
        num, den = num_den(total, t, share, tokens)
        summaries.append(num / den)
    inverses = [inverse_norm(summary) for summary in summaries]
    pooled = [summary * inverse for summary, inverse in zip(summaries, inverses)]
    weights = [jnp.exp(scale * close_dot(pooled[t], units[t], 1, 1)) for t in steps]
    attention = [weight / jnp.sum(weight, axis=0, keepdims=True) for weight in weights]
    blended = [rounded_dot(attention[t], summaries[t], 0, 0) for t in steps]
    blended_inverses = [inverse_norm(each) for each in blended]
    normed = [each * inverse for each, inverse in zip(blended, blended_inverses)]
    d_blended = [
        normalize_back(
            blended_inverses[t], normed[t], ready_ref[2, t * n_rows : (t + 1) * n_rows, :]
        )
        for t in steps
    ]
    d_attention = [close_dot(summaries[t], d_blended[t], 1, 1) for t in steps]
    d_scores = [
        attention[t]
        * (d_attention[t] - jnp.sum(attention[t] * d_attention[t], axis=0, keepdims=True))
        for t in steps
    ]
    d_pooled = [scale * rounded_dot(d_scores[t], units[t], 1, 0) for t in steps]
    direct = [close_dot(attention[t], d_blended[t], 1, 0) for t in steps]
    for t in steps:
        own = slice(t * tokens, (t + 1) * tokens)
        ds_ref[own, :] = direct[t] + normalize_back(inverses[t], pooled[t], d_pooled[t])
        d_scores_ref[own, :] = d_scores[t]
        normed_ref[t * n_rows : (t + 1) * n_rows, :] = normed[t].astype(bf16)


def query_kernel(share, sensors, terms, swapped, wq, wo, ready_ref, normed_ref, d_scores_ref, *refs):
    sums, (lay_ref, dh_ref) = refs[:terms], refs[terms:]
    width = wq.shape[0]
    tokens = d_scores_ref.shape[0] // share
    scale = scale_of(width)
    total = total_of(sums)
    n_rows = ready_ref.shape[1] // share
    grad_rows = share * n_rows
    for t in range(share):
        at = slice(t * n_rows, (t + 1) * n_rows)
        rows = rows_of(swapped, t, sensors)
        cotangent = rows_of(swapped, share + t, sensors)
        normed = normed_ref[at, :]
        layer = (rows + dot(normed, wo[...], 1, 0)).astype(bf16).astype(f32)
        put_rows(lay_ref, t, sensors, layer)
        grad_out = dot(normed, cotangent.astype(bf16), 0, 0)
        num, den = num_den(total, t, share, tokens)
        summary = num / den
        pooled = summary * inverse_norm(summary)
        d_unit = scale * close_dot(d_scores_ref[t * tokens : (t + 1) * tokens, :], pooled, 0, 0)
        d_query = normalize_back(ready_ref[1, at, :], ready_ref[0, at, :], d_unit).astype(bf16)
        grad_query = dot(rows.astype(bf16), d_query, 0, 0)
        dh_ref[at, :] = cotangent + dot(d_query, wq[...], 1, 1)
        for i, grad in enumerate((grad_query, grad_out)):
            to = slice(grad_rows + i * width, grad_rows + (i + 1) * width)
            dh_ref[to, :] = grad if t == 0 else dh_ref[to, :] + grad


def put_partials(ref, grads):
    owners, rows, width = ref.shape
    for m in range(owners):
        at = 0
        for grad in grads:
            own = grad.shape[0] // owners
            ref[m, at : at + own, :] = grad[m * own : (m + 1) * own, :]
            at += own
        if at < rows:
            ref[m, at:, :] = jnp.zeros((rows - at, width), f32)


def in_back_kernel(
    share, sensors, terms, swapped, projector, wk, wv, ready_ref, dh_ref, layer_ref, *refs
):
    sums, d_sums = refs[:terms], refs[terms : 2 * terms]
    far_ref, part_ref, out_ref, sems = refs[2 * terms :]
    half = share * sensors
    sent = [pltpu.make_async_copy(layer_ref, far_ref.at[:, pl.ds(0, half)], sems.at[share])]
    sent[0].start()
    tokens, width = projector.shape
    scale = scale_of(width)
    total = total_of(sums)
    d_total = total_of(d_sums)
    mapping_inverse = inverse_norm(projector[...])
    mapping = projector[...] * mapping_inverse
    turned = jnp.concatenate([wk[...], wv[...]], axis=1)
    n_rows = ready_ref.shape[1] // share
    grad_rows = share * n_rows
    steps = range(share)
    spans = [slice(t * n_rows, (t + 1) * n_rows) for t in steps]
    hidden = [rows_of(swapped, t, sensors).astype(bf16) for t in steps]
    units = [ready_ref[0, span, :] for span in spans]
    weights = [
        jnp.concatenate(
            [
                ready_ref[3, t * n_rows + i * tokens : t * n_rows + (i + 1) * tokens, :]
                for i in range(n_rows // width)
            ],
            axis=1,
        )
        for t in steps
    ]
    d_nums, d_dens = [], []
    for t in steps:
        num, den = num_den(total, t, share, tokens)
        d_summary = d_total[t * tokens : (t + 1) * tokens, :]
        d_nums.append(d_summary / den)
        d_dens.append(-jnp.sum(d_summary * num, axis=1, keepdims=True) / (den * den))
    d_weights = []
    for t in steps:
        high, low = split(d_nums[t])
        values = ready_ref[2, spans[t], :].astype(bf16)
        d_weights.append(dot(high, values, 1, 1) + dot(low, values, 1, 1) + d_dens[t])
    d_scores = [d_weights[t] * weights[t] for t in steps]
    d_units = [scale * rounded_dot(d_scores[t], mapping, 0, 0) for t in steps]
    d_values = [rounded_dot(weights[t], d_nums[t], 0, 0).astype(bf16) for t in steps]
    d_keys = [
        normalize_back(ready_ref[1, spans[t], :], units[t], d_units[t]).astype(bf16) for t in steps
    ]
    together = [jnp.concatenate([d_keys[t], d_values[t]], axis=1) for t in steps]
    for t in steps:
        put_rows(out_ref, t, sensors, dh_ref[spans[t], :] + dot(together[t], turned, 1, 1))
        copy = pltpu.make_async_copy(
            out_ref.at[:, pl.ds(t * sensors, sensors)],
            far_ref.at[:, pl.ds(half + t * sensors, sensors)],
            sems.at[t],
        )
        copy.start()
        sent.append(copy)
    d_mapping = sum(scale * rounded_dot(d_scores[t], units[t], 1, 0) for t in steps)
    gradients = sum(dot(hidden[t], together[t], 0, 0) for t in steps)
    parts = [normalize_back(mapping_inverse, mapping, d_mapping)]
    parts += [gradients[:, :width], gradients[:, width:]]
    parts += [dh_ref[grad_rows + i * width : grad_rows + (i + 1) * width, :] for i in range(2)]
    put_partials(part_ref, parts)
    for copy in sent:
        copy.wait()


def deal_kernel(count, place_ref, *refs):
    chunks, out_refs, rows = refs[:count], refs[count:-1], refs[-1]
    for m, chunk in enumerate(chunks):
        source = lax.bitwise_xor(place_ref[0], m)
        rows[pl.ds(source * chunk.shape[0], chunk.shape[0]), :] = chunk[...]
    at = 0
    for out in out_refs:
        out[...] = rows[at : at + out.shape[0], :]
        at += out.shape[0]


def call(kernel, out_shape, *args, vmem=32, **more):
    return pl.pallas_call(kernel, out_shape=out_shape, compiler_params=params(vmem), **more)(*args)


def group_size(most, *sizes):
    group = 1
    while group < most and all(size % (2 * group) == 0 for size in sizes):
        group *= 2
    return group


def per_device(n_sensor, n_tm, inputs, mask, projector, w_key, w_value, w_query, w_out, cotangent):
    sensors, steps, width = inputs.shape
    tokens = projector.shape[0]
    group = group_size(8, n_sensor, steps)
    rest = n_sensor // group
    share = steps // group
    blocks = [list(range(r * group, (r + 1) * group)) for r in range(rest)]

    def swap(rows):
        return lax.all_to_all(rows, "sensor", 0, 0, tiled=True, axis_index_groups=blocks)

    def others(rows):
        return [
            lax.ppermute(
                rows, "sensor", [(i, (i + step * group) % n_sensor) for i in range(n_sensor)]
            )
            for step in range(1, rest)
        ]

    def shape(*dims, kind=f32):
        return jax.ShapeDtypeStruct(dims, kind)

    wide = pltpu.VMEM(inputs.shape, f32)
    mask = mask.T

    place_spec = pl.BlockSpec(memory_space=pltpu.SMEM)
    far_spec = pl.BlockSpec(memory_space=pltpu.HBM)
    near_spec = pl.BlockSpec(memory_space=pltpu.VMEM)
    swapped = swap(
        call(
            outward_kernel,
            shape(group, 2 * share * sensors, width),
            inputs, mask, cotangent,
            vmem=60,
            in_specs=[far_spec, near_spec, far_spec],
            out_specs=far_spec,
            scratch_shapes=[
                pltpu.VMEM(inputs.shape, bf16),
                pltpu.VMEM(inputs.shape, bf16),
                wide,
                pltpu.VMEM((group, 2 * share * sensors, width), f32),
                pltpu.SemaphoreType.DMA((2 * group + 2,)),
            ],
        )
    )
    n_rows = group * sensors
    sums_rows = share * tokens + -(-share // 8) * 8
    sums = call(
        functools.partial(in_kernel, share, sensors),
        shape(sums_rows, width),
        swapped, projector, w_key, w_value,
    )
    sums = [sums] + others(sums)
    tokens_shape = shape(share * tokens, n_rows)
    owned = [tokens // n_tm] + [width // n_tm] * 4
    quarter = group_size(4, n_sensor)
    chunk = -(-sum(owned) // (8 * quarter)) * 8
    ready_in, ready_out = call(
        functools.partial(ready_kernel, share, sensors),
        (shape(4, share * n_rows, width), shape(3, share * n_rows, width)),
        swapped, projector, w_key, w_value, w_query, w_out,
    )
    d_sums, normed, d_scores = call(
        functools.partial(out_kernel, share, rest),
        (shape(share * tokens, width), shape(share * n_rows, width, kind=bf16), tokens_shape),
        ready_out, *sums,
    )
    d_sums = [d_sums] + others(d_sums)
    layer, d_hidden = call(
        functools.partial(query_kernel, share, sensors, rest),
        (
            shape(group, share * sensors, width),
            shape(share * n_rows + 2 * width, width),
        ),
        swapped, w_query, w_out, ready_out, normed, d_scores, *sums,
    )
    back, part = call(
        functools.partial(in_back_kernel, share, sensors, rest),
        (
            shape(group, 2 * share * sensors, width),
            shape(n_tm, quarter * chunk, width),
        ),
        swapped, projector, w_key, w_value, ready_in, d_hidden, layer, *sums, *d_sums,
        out_specs=(far_spec, near_spec),
        scratch_shapes=[
            pltpu.VMEM((group, share * sensors, width), f32),
            pltpu.SemaphoreType.DMA((share + 1,)),
        ],
    )
    me = lax.axis_index("tm")
    mine = lax.dynamic_index_in_dim(part, me, 0, keepdims=False)
    for step in range(1, n_tm):
        gone = lax.dynamic_index_in_dim(part, lax.rem(me + step, n_tm), 0, keepdims=False)
        ring = [(i, (i + step) % n_tm) for i in range(n_tm)]
        mine = mine + lax.ppermute(gone, "tm", ring)

    def partner(rows, m):
        return lax.ppermute(rows, "sensor", [(i, i ^ m) for i in range(n_sensor)])

    mine = mine.reshape(quarter, chunk, width)
    place = lax.rem(lax.axis_index("sensor"), quarter)
    total = lax.dynamic_index_in_dim(mine, place, 0, keepdims=False)
    for m in range(1, quarter):
        gone = lax.dynamic_index_in_dim(mine, lax.bitwise_xor(place, m), 0, keepdims=False)
        total = total + partner(gone, m)
    home = swap(back)
    output_rows, d_inputs = call(
        homeward_kernel,
        (shape(*inputs.shape, kind=bf16), shape(*inputs.shape, kind=bf16)),
        home, mask,
        scratch_shapes=[wide, wide],
    )
    m = quarter
    while n_sensor % (2 * m) == 0:
        gone = partner(total, m)
        m *= 2
        if n_sensor % (2 * m):
            total, gone, output_rows, d_inputs = lax.optimization_barrier(
                (total, gone, output_rows, d_inputs)
            )
        total = total + gone
    odd = n_sensor // m
    spread = [
        lax.ppermute(total, "sensor", [(i, (i + step * m) % n_sensor) for i in range(n_sensor)])
        for step in range(1, odd)
    ]
    total = sum(spread, total)
    chunks = [total] + [partner(total, m) for m in range(1, quarter)]
    outs = call(
        functools.partial(deal_kernel, quarter),
        tuple(shape(n, width) for n in owned),
        place[None], *chunks,
        in_specs=[place_spec] + [near_spec] * quarter,
        scratch_shapes=[pltpu.VMEM((quarter * chunk, width), f32)],
    )
    return (output_rows, d_inputs, *outs)


def solution(mesh):
    placed = (
        P("sensor", "tm", None),
        P("sensor", "tm"),
        P(),
        P(),
        P(),
        P(),
        P(),
        P("sensor", "tm", None),
    )
    return jax.shard_map(
        functools.partial(per_device, mesh.shape["sensor"], mesh.shape["tm"]),
        mesh=mesh,
        in_specs=placed,
        out_specs=(
            P("sensor", "tm", None),
            P("sensor", "tm", None),
            P("tm", None),
            P("tm", None),
            P("tm", None),
            P("tm", None),
            P("tm", None),
        ),
        check_vma=False,
    )
```

```python
import functools

import jax
import jax.numpy as jnp
from jax import lax
from jax.experimental import pallas as pl
from jax.experimental.pallas import tpu as pltpu
from jax.sharding import PartitionSpec as P

sharpness_divisor = 12.0
epsilon = 1e-06
f32 = jnp.float32
bf16 = jnp.bfloat16


def params(mebibytes=32):
    return pltpu.CompilerParams(vmem_limit_bytes=mebibytes * 1024 * 1024)


def dot(left, right, left_dim, right_dim):
    return lax.dot_general(
        left, right, (((left_dim,), (right_dim,)), ((), ())), preferred_element_type=f32
    )


def rounded_dot(left, right, left_dim, right_dim):
    return dot(left.astype(bf16), right.astype(bf16), left_dim, right_dim)


def split(value):
    high = value.astype(bf16)
    return high, (value - high.astype(f32)).astype(bf16)


def close_dot(left, right, left_dim, right_dim):
    high, low = split(left)
    right_high, right_low = split(right)
    return (
        dot(high, right_high, left_dim, right_dim)
        + dot(high, right_low, left_dim, right_dim)
        + dot(low, right_high, left_dim, right_dim)
    )


def inverse_norm(vector):
    return lax.rsqrt(jnp.mean(vector * vector, axis=-1, keepdims=True) + epsilon)


def normalize_back(inverse, unit, gradient):
    return inverse * (gradient - unit * jnp.mean(unit * gradient, axis=-1, keepdims=True))


def diagonal(tokens):
    rows = lax.broadcasted_iota(jnp.int32, (tokens, tokens), 0)
    return rows == lax.broadcasted_iota(jnp.int32, (tokens, tokens), 1)


def turned_mask(mask_ref):
    sensors = mask_ref.shape[1]
    return dot(diagonal(sensors).astype(f32).astype(bf16), mask_ref[...].astype(f32).astype(bf16), 1, 1)


def outward_kernel(
    inputs_ref, mask_ref, cotangent_ref, far_ref, near, near_mask, near_cotangent, wide, out_ref, sems
):
    sensors, steps, _ = inputs_ref.shape
    places = out_ref.shape[0]
    share = steps // places
    rows = share * sensors
    first = pltpu.make_async_copy(inputs_ref, near, sems.at[2 * places])
    second = pltpu.make_async_copy(cotangent_ref, near_cotangent, sems.at[2 * places + 1])
    third = pltpu.make_async_copy(mask_ref, near_mask, sems.at[2 * places + 2])
    first.start()
    third.start()
    second.start()
    sent = []

    def send(place, half):
        block = (place, pl.ds(half * rows, rows))
        copy = pltpu.make_async_copy(
            out_ref.at[block], far_ref.at[block], sems.at[half * places + place]
        )
        copy.start()
        sent.append(copy)

    third.wait()
    marks = turned_mask(near_mask)
    first.wait()
    wide[...] = near[...].astype(f32)
    for place in range(places):
        for own in range(share):
            t = place * share + own
            out_ref[place, own * sensors : (own + 1) * sensors, :] = (
                wide[:, t, :] * marks[:, t : t + 1]
            )
        send(place, 0)
    second.wait()
    wide[...] = near_cotangent[...].astype(f32)
    for place in range(places):
        for own in range(share):
            at = rows + own * sensors
            out_ref[place, at : at + sensors, :] = wide[:, place * share + own, :]
        send(place, 1)
    for copy in sent:
        copy.wait()


def homeward_kernel(rows_ref, mask_ref, layer_ref, d_inputs_ref, wide, wide_gradient):
    sensors, steps, _ = layer_ref.shape
    share = steps // rows_ref.shape[0]
    marks = turned_mask(mask_ref)
    for t in range(steps):
        place, own = divmod(t, share)
        wide[:, t, :] = rows_ref[place, own * sensors : (own + 1) * sensors, :]
        at = (share + own) * sensors
        wide_gradient[:, t, :] = rows_ref[place, at : at + sensors, :] * marks[:, t : t + 1]
    layer_ref[...] = wide[...].astype(bf16)
    d_inputs_ref[...] = wide_gradient[...].astype(bf16)


def rows_of(ref, block, sensors):
    rows = ref[:, block * sensors : (block + 1) * sensors, :]
    return rows.reshape(rows.shape[0] * sensors, rows.shape[2])


def put_rows(ref, block, sensors, rows):
    ref[:, block * sensors : (block + 1) * sensors, :] = rows.reshape(
        ref.shape[0], sensors, rows.shape[1]
    )


def scale_of(width):
    return sharpness_divisor / width


def weigh_in(key_raw, projector):
    inverse = inverse_norm(key_raw)
    unit = key_raw * inverse
    mapping = projector * inverse_norm(projector)
    scale = scale_of(key_raw.shape[-1])
    return inverse, unit, jnp.exp(scale * close_dot(mapping, unit, 1, 1))


def in_kernel(share, sensors, swapped, projector, wk, wv, sums_ref):
    tokens, width = projector.shape
    same = diagonal(tokens)
    tail = share * tokens
    sums_ref[tail:, :] = jnp.zeros((sums_ref.shape[0] - tail, width), f32)
    both_weights = jnp.concatenate([wk[...], wv[...]], axis=1)
    steps = range(share)
    both = [dot(rows_of(swapped, t, sensors).astype(bf16), both_weights, 1, 0) for t in steps]
    weights = [weigh_in(raw[:, :width], projector[...])[2] for raw in both]
    dens = [jnp.sum(weight, axis=1, keepdims=True) for weight in weights]
    nums = [rounded_dot(weights[t], both[t][:, width:], 1, 0) for t in steps]
    for t in steps:
        sums_ref[t * tokens : (t + 1) * tokens, :] = nums[t]
        sums_ref[tail + t : tail + t + 1, :tokens] = jnp.sum(
            jnp.where(same, dens[t], 0.0), axis=0, keepdims=True
        )


def total_of(refs):
    total = refs[0][...]
    for ref in refs[1:]:
        total = total + ref[...]
    return total


def num_den(total, t, share, tokens):
    num = total[t * tokens : (t + 1) * tokens, :]
    at = share * tokens + t
    den = jnp.sum(
        jnp.where(diagonal(tokens), total[at : at + 1, :tokens], 0.0), axis=1, keepdims=True
    )
    return num, den


def ready_kernel(
    share, sensors, swapped, projector, wk, wv, wq, wo,
    in_ref, out_ref,
):
    width = wk.shape[0]
    tokens = projector.shape[0]
    together = jnp.concatenate([wk[...], wv[...], wq[...]], axis=1)
    for t in range(share):
        hidden = rows_of(swapped, t, sensors).astype(bf16)
        at = slice(t * hidden.shape[0], (t + 1) * hidden.shape[0])
        raw = dot(hidden, together, 1, 0)
        inverse, unit, weights = weigh_in(raw[:, :width], projector[...])
        query_raw = raw[:, 2 * width :]
        query_inverse = inverse_norm(query_raw)
        in_ref[0, at, :] = unit
        in_ref[1, at, :] = jnp.broadcast_to(inverse, unit.shape)
        in_ref[2, at, :] = raw[:, width : 2 * width].astype(bf16).astype(f32)
        for block in range(hidden.shape[0] // width):
            to = block * tokens + t * hidden.shape[0]
            in_ref[3, to : to + tokens, :] = weights[:, block * width : (block + 1) * width]
        out_ref[0, at, :] = query_raw * query_inverse
        out_ref[1, at, :] = jnp.broadcast_to(query_inverse, unit.shape)
        cotangent = rows_of(swapped, share + t, sensors).astype(bf16)
        out_ref[2, at, :] = dot(cotangent, wo[...], 1, 1).astype(bf16).astype(f32)


def out_kernel(share, terms, ready_ref, *refs):
    sums, (ds_ref, normed_ref, d_scores_ref) = refs[:terms], refs[terms:]
    width = ready_ref.shape[2]
    tokens = ds_ref.shape[0] // share
    scale = scale_of(width)
    total = total_of(sums)
    n_rows = ready_ref.shape[1] // share
    steps = range(share)
    units = [ready_ref[0, t * n_rows : (t + 1) * n_rows, :] for t in steps]
    summaries = []
    for t in steps:
        num, den = num_den(total, t, share, tokens)
        summaries.append(num / den)
    inverses = [inverse_norm(summary) for summary in summaries]
    pooled = [summary * inverse for summary, inverse in zip(summaries, inverses)]
    weights = [jnp.exp(scale * close_dot(pooled[t], units[t], 1, 1)) for t in steps]
    attention = [weight / jnp.sum(weight, axis=0, keepdims=True) for weight in weights]
    blended = [rounded_dot(attention[t], summaries[t], 0, 0) for t in steps]
    blended_inverses = [inverse_norm(each) for each in blended]
    normed = [each * inverse for each, inverse in zip(blended, blended_inverses)]
    d_blended = [
        normalize_back(
            blended_inverses[t], normed[t], ready_ref[2, t * n_rows : (t + 1) * n_rows, :]
        )
        for t in steps
    ]
    d_attention = [close_dot(summaries[t], d_blended[t], 1, 1) for t in steps]
    d_scores = [
        attention[t]
        * (d_attention[t] - jnp.sum(attention[t] * d_attention[t], axis=0, keepdims=True))
        for t in steps
    ]
    d_pooled = [scale * rounded_dot(d_scores[t], units[t], 1, 0) for t in steps]
    direct = [close_dot(attention[t], d_blended[t], 1, 0) for t in steps]
    for t in steps:
        own = slice(t * tokens, (t + 1) * tokens)
        ds_ref[own, :] = direct[t] + normalize_back(inverses[t], pooled[t], d_pooled[t])
        d_scores_ref[own, :] = d_scores[t]
        normed_ref[t * n_rows : (t + 1) * n_rows, :] = normed[t].astype(bf16)


def query_kernel(share, sensors, terms, swapped, wq, wo, ready_ref, normed_ref, d_scores_ref, *refs):
    sums, (lay_ref, dh_ref) = refs[:terms], refs[terms:]
    width = wq.shape[0]
    tokens = d_scores_ref.shape[0] // share
    scale = scale_of(width)
    total = total_of(sums)
    n_rows = ready_ref.shape[1] // share
    grad_rows = share * n_rows
    for t in range(share):
        at = slice(t * n_rows, (t + 1) * n_rows)
        rows = rows_of(swapped, t, sensors)
        cotangent = rows_of(swapped, share + t, sensors)
        normed = normed_ref[at, :]
        layer = (rows + dot(normed, wo[...], 1, 0)).astype(bf16).astype(f32)
        put_rows(lay_ref, t, sensors, layer)
        grad_out = dot(normed, cotangent.astype(bf16), 0, 0)
        num, den = num_den(total, t, share, tokens)
        summary = num / den
        pooled = summary * inverse_norm(summary)
        d_unit = scale * close_dot(d_scores_ref[t * tokens : (t + 1) * tokens, :], pooled, 0, 0)
        d_query = normalize_back(ready_ref[1, at, :], ready_ref[0, at, :], d_unit).astype(bf16)
        grad_query = dot(rows.astype(bf16), d_query, 0, 0)
        dh_ref[at, :] = cotangent + dot(d_query, wq[...], 1, 1)
        for i, grad in enumerate((grad_query, grad_out)):
            to = slice(grad_rows + i * width, grad_rows + (i + 1) * width)
            dh_ref[to, :] = grad if t == 0 else dh_ref[to, :] + grad


def put_partials(ref, grads):
    owners, rows, width = ref.shape
    for m in range(owners):
        at = 0
        for grad in grads:
            own = grad.shape[0] // owners
            ref[m, at : at + own, :] = grad[m * own : (m + 1) * own, :]
            at += own
        if at < rows:
            ref[m, at:, :] = jnp.zeros((rows - at, width), f32)


def in_back_kernel(
    share, sensors, terms, swapped, projector, wk, wv, ready_ref, dh_ref, layer_ref, *refs
):
    sums, d_sums = refs[:terms], refs[terms : 2 * terms]
    far_ref, part_ref, out_ref, sems = refs[2 * terms :]
    half = share * sensors
    sent = [pltpu.make_async_copy(layer_ref, far_ref.at[:, pl.ds(0, half)], sems.at[share])]
    sent[0].start()
    tokens, width = projector.shape
    scale = scale_of(width)
    total = total_of(sums)
    d_total = total_of(d_sums)
    mapping_inverse = inverse_norm(projector[...])
    mapping = projector[...] * mapping_inverse
    turned = jnp.concatenate([wk[...], wv[...]], axis=1)
    n_rows = ready_ref.shape[1] // share
    grad_rows = share * n_rows
    steps = range(share)
    spans = [slice(t * n_rows, (t + 1) * n_rows) for t in steps]
    hidden = [rows_of(swapped, t, sensors).astype(bf16) for t in steps]
    units = [ready_ref[0, span, :] for span in spans]
    weights = [
        jnp.concatenate(
            [
                ready_ref[3, t * n_rows + i * tokens : t * n_rows + (i + 1) * tokens, :]
                for i in range(n_rows // width)
            ],
            axis=1,
        )
        for t in steps
    ]
    d_nums, d_dens = [], []
    for t in steps:
        num, den = num_den(total, t, share, tokens)
        d_summary = d_total[t * tokens : (t + 1) * tokens, :]
        d_nums.append(d_summary / den)
        d_dens.append(-jnp.sum(d_summary * num, axis=1, keepdims=True) / (den * den))
    d_weights = []
    for t in steps:
        high, low = split(d_nums[t])
        values = ready_ref[2, spans[t], :].astype(bf16)
        d_weights.append(dot(high, values, 1, 1) + dot(low, values, 1, 1) + d_dens[t])
    d_scores = [d_weights[t] * weights[t] for t in steps]
    d_units = [scale * rounded_dot(d_scores[t], mapping, 0, 0) for t in steps]
    d_values = [rounded_dot(weights[t], d_nums[t], 0, 0).astype(bf16) for t in steps]
    d_keys = [
        normalize_back(ready_ref[1, spans[t], :], units[t], d_units[t]).astype(bf16) for t in steps
    ]
    together = [jnp.concatenate([d_keys[t], d_values[t]], axis=1) for t in steps]
    for t in steps:
        put_rows(out_ref, t, sensors, dh_ref[spans[t], :] + dot(together[t], turned, 1, 1))
        copy = pltpu.make_async_copy(
            out_ref.at[:, pl.ds(t * sensors, sensors)],
            far_ref.at[:, pl.ds(half + t * sensors, sensors)],
            sems.at[t],
        )
        copy.start()
        sent.append(copy)
    d_mapping = sum(scale * rounded_dot(d_scores[t], units[t], 1, 0) for t in steps)
    gradients = sum(dot(hidden[t], together[t], 0, 0) for t in steps)
    parts = [normalize_back(mapping_inverse, mapping, d_mapping)]
    parts += [gradients[:, :width], gradients[:, width:]]
    parts += [dh_ref[grad_rows + i * width : grad_rows + (i + 1) * width, :] for i in range(2)]
    put_partials(part_ref, parts)
    for copy in sent:
        copy.wait()


def deal_kernel(count, place_ref, *refs):
    chunks, out_refs, rows = refs[:count], refs[count:-1], refs[-1]
    for m, chunk in enumerate(chunks):
        source = lax.bitwise_xor(place_ref[0], m)
        rows[pl.ds(source * chunk.shape[0], chunk.shape[0]), :] = chunk[...]
    at = 0
    for out in out_refs:
        out[...] = rows[at : at + out.shape[0], :]
        at += out.shape[0]


def call(kernel, out_shape, *args, vmem=32, **more):
    return pl.pallas_call(kernel, out_shape=out_shape, compiler_params=params(vmem), **more)(*args)


def group_size(most, *sizes):
    group = 1
    while group < most and all(size % (2 * group) == 0 for size in sizes):
        group *= 2
    return group


def per_device(n_sensor, n_tm, inputs, mask, projector, w_key, w_value, w_query, w_out, cotangent):
    sensors, steps, width = inputs.shape
    tokens = projector.shape[0]
    group = group_size(8, n_sensor, steps)
    rest = n_sensor // group
    share = steps // group
    blocks = [list(range(r * group, (r + 1) * group)) for r in range(rest)]

    def swap(rows):
        return lax.all_to_all(rows, "sensor", 0, 0, tiled=True, axis_index_groups=blocks)

    def others(rows):
        return [
            lax.ppermute(
                rows, "sensor", [(i, (i + step * group) % n_sensor) for i in range(n_sensor)]
            )
            for step in range(1, rest)
        ]

    def shape(*dims, kind=f32):
        return jax.ShapeDtypeStruct(dims, kind)

    wide = pltpu.VMEM(inputs.shape, f32)
    mask = mask.T

    place_spec = pl.BlockSpec(memory_space=pltpu.SMEM)
    far_spec = pl.BlockSpec(memory_space=pltpu.HBM)
    near_spec = pl.BlockSpec(memory_space=pltpu.VMEM)
    swapped = swap(
        call(
            outward_kernel,
            shape(group, 2 * share * sensors, width),
            inputs, mask, cotangent,
            vmem=60,
            in_specs=[far_spec, far_spec, far_spec],
            out_specs=far_spec,
            scratch_shapes=[
                pltpu.VMEM(inputs.shape, bf16),
                pltpu.VMEM(mask.shape, mask.dtype),
                pltpu.VMEM(inputs.shape, bf16),
                wide,
                pltpu.VMEM((group, 2 * share * sensors, width), f32),
                pltpu.SemaphoreType.DMA((2 * group + 3,)),
            ],
        )
    )
    n_rows = group * sensors
    sums_rows = share * tokens + -(-share // 8) * 8
    sums = call(
        functools.partial(in_kernel, share, sensors),
        shape(sums_rows, width),
        swapped, projector, w_key, w_value,
    )
    sums = [sums] + others(sums)
    tokens_shape = shape(share * tokens, n_rows)
    owned = [tokens // n_tm] + [width // n_tm] * 4
    quarter = group_size(4, n_sensor)
    chunk = -(-sum(owned) // (8 * quarter)) * 8
    ready_in, ready_out = call(
        functools.partial(ready_kernel, share, sensors),
        (shape(4, share * n_rows, width), shape(3, share * n_rows, width)),
        swapped, projector, w_key, w_value, w_query, w_out,
    )
    d_sums, normed, d_scores = call(
        functools.partial(out_kernel, share, rest),
        (shape(share * tokens, width), shape(share * n_rows, width, kind=bf16), tokens_shape),
        ready_out, *sums,
    )
    d_sums = [d_sums] + others(d_sums)
    layer, d_hidden = call(
        functools.partial(query_kernel, share, sensors, rest),
        (
            shape(group, share * sensors, width),
            shape(share * n_rows + 2 * width, width),
        ),
        swapped, w_query, w_out, ready_out, normed, d_scores, *sums,
    )
    back, part = call(
        functools.partial(in_back_kernel, share, sensors, rest),
        (
            shape(group, 2 * share * sensors, width),
            shape(n_tm, quarter * chunk, width),
        ),
        swapped, projector, w_key, w_value, ready_in, d_hidden, layer, *sums, *d_sums,
        out_specs=(far_spec, near_spec),
        scratch_shapes=[
            pltpu.VMEM((group, share * sensors, width), f32),
            pltpu.SemaphoreType.DMA((share + 1,)),
        ],
    )
    me = lax.axis_index("tm")
    mine = lax.dynamic_index_in_dim(part, me, 0, keepdims=False)
    for step in range(1, n_tm):
        gone = lax.dynamic_index_in_dim(part, lax.rem(me + step, n_tm), 0, keepdims=False)
        ring = [(i, (i + step) % n_tm) for i in range(n_tm)]
        mine = mine + lax.ppermute(gone, "tm", ring)

    def partner(rows, m):
        return lax.ppermute(rows, "sensor", [(i, i ^ m) for i in range(n_sensor)])

    mine = mine.reshape(quarter, chunk, width)
    place = lax.rem(lax.axis_index("sensor"), quarter)
    total = lax.dynamic_index_in_dim(mine, place, 0, keepdims=False)
    for m in range(1, quarter):
        gone = lax.dynamic_index_in_dim(mine, lax.bitwise_xor(place, m), 0, keepdims=False)
        total = total + partner(gone, m)
    home = swap(back)
    output_rows, d_inputs = call(
        homeward_kernel,
        (shape(*inputs.shape, kind=bf16), shape(*inputs.shape, kind=bf16)),
        home, mask,
        scratch_shapes=[wide, wide],
    )
    m = quarter
    while n_sensor % (2 * m) == 0:
        gone = partner(total, m)
        m *= 2
        if n_sensor % (2 * m):
            total, gone, output_rows, d_inputs = lax.optimization_barrier(
                (total, gone, output_rows, d_inputs)
            )
        total = total + gone
    odd = n_sensor // m
    spread = [
        lax.ppermute(total, "sensor", [(i, (i + step * m) % n_sensor) for i in range(n_sensor)])
        for step in range(1, odd)
    ]
    total = sum(spread, total)
    chunks = [total] + [partner(total, m) for m in range(1, quarter)]
    outs = call(
        functools.partial(deal_kernel, quarter),
        tuple(shape(n, width) for n in owned),
        place[None], *chunks,
        in_specs=[place_spec] + [near_spec] * quarter,
        scratch_shapes=[pltpu.VMEM((quarter * chunk, width), f32)],
    )
    return (output_rows, d_inputs, *outs)


def solution(mesh):
    placed = (
        P("sensor", "tm", None),
        P("sensor", "tm"),
        P(),
        P(),
        P(),
        P(),
        P(),
        P("sensor", "tm", None),
    )
    return jax.shard_map(
        functools.partial(per_device, mesh.shape["sensor"], mesh.shape["tm"]),
        mesh=mesh,
        in_specs=placed,
        out_specs=(
            P("sensor", "tm", None),
            P("sensor", "tm", None),
            P("tm", None),
            P("tm", None),
            P("tm", None),
            P("tm", None),
            P("tm", None),
        ),
        check_vma=False,
    )
```

```python
import functools

import jax
import jax.numpy as jnp
from jax import lax
from jax.experimental import pallas as pl
from jax.experimental.pallas import tpu as pltpu
from jax.sharding import PartitionSpec as P

sharpness_divisor = 12.0
epsilon = 1e-06
f32 = jnp.float32
bf16 = jnp.bfloat16


def params(mebibytes=32):
    return pltpu.CompilerParams(vmem_limit_bytes=mebibytes * 1024 * 1024)


def dot(left, right, left_dim, right_dim):
    return lax.dot_general(
        left, right, (((left_dim,), (right_dim,)), ((), ())), preferred_element_type=f32
    )


def rounded_dot(left, right, left_dim, right_dim):
    return dot(left.astype(bf16), right.astype(bf16), left_dim, right_dim)


def split(value):
    high = value.astype(bf16)
    return high, (value - high.astype(f32)).astype(bf16)


def close_dot(left, right, left_dim, right_dim):
    high, low = split(left)
    right_high, right_low = split(right)
    return dot(
        jnp.concatenate([high, high, low], axis=left_dim),
        jnp.concatenate([right_high, right_low, right_high], axis=right_dim),
        left_dim,
        right_dim,
    )


def inverse_norm(vector):
    return lax.rsqrt(jnp.mean(vector * vector, axis=-1, keepdims=True) + epsilon)


def normalize_back(inverse, unit, gradient):
    return inverse * (gradient - unit * jnp.mean(unit * gradient, axis=-1, keepdims=True))


def diagonal(tokens):
    rows = lax.broadcasted_iota(jnp.int32, (tokens, tokens), 0)
    return rows == lax.broadcasted_iota(jnp.int32, (tokens, tokens), 1)


def turned_mask(mask_ref):
    sensors = mask_ref.shape[1]
    return dot(diagonal(sensors).astype(f32).astype(bf16), mask_ref[...].astype(f32).astype(bf16), 1, 1)


def outward_kernel(
    inputs_ref, mask_ref, cotangent_ref, far_ref, near, near_mask, near_cotangent, wide, out_ref, sems
):
    sensors, steps, _ = inputs_ref.shape
    places = out_ref.shape[0]
    share = steps // places
    rows = share * sensors
    first = pltpu.make_async_copy(inputs_ref, near, sems.at[2 * places])
    second = pltpu.make_async_copy(cotangent_ref, near_cotangent, sems.at[2 * places + 1])
    third = pltpu.make_async_copy(mask_ref, near_mask, sems.at[2 * places + 2])
    first.start()
    third.start()
    second.start()
    sent = []

    def send(place, half):
        block = (place, pl.ds(half * rows, rows))
        copy = pltpu.make_async_copy(
            out_ref.at[block], far_ref.at[block], sems.at[half * places + place]
        )
        copy.start()
        sent.append(copy)

    third.wait()
    marks = turned_mask(near_mask)
    first.wait()
    wide[...] = near[...].astype(f32)
    for place in range(places):
        for own in range(share):
            t = place * share + own
            out_ref[place, own * sensors : (own + 1) * sensors, :] = (
                wide[:, t, :] * marks[:, t : t + 1]
            )
        send(place, 0)
    second.wait()
    wide[...] = near_cotangent[...].astype(f32)
    for place in range(places):
        for own in range(share):
            at = rows + own * sensors
            out_ref[place, at : at + sensors, :] = wide[:, place * share + own, :]
        send(place, 1)
    for copy in sent:
        copy.wait()


def homeward_kernel(rows_ref, mask_ref, layer_ref, d_inputs_ref, wide, wide_gradient):
    sensors, steps, _ = layer_ref.shape
    share = steps // rows_ref.shape[0]
    marks = turned_mask(mask_ref)
    for t in range(steps):
        place, own = divmod(t, share)
        wide[:, t, :] = rows_ref[place, own * sensors : (own + 1) * sensors, :]
        at = (share + own) * sensors
        wide_gradient[:, t, :] = rows_ref[place, at : at + sensors, :] * marks[:, t : t + 1]
    layer_ref[...] = wide[...].astype(bf16)
    d_inputs_ref[...] = wide_gradient[...].astype(bf16)


def rows_of(ref, block, sensors):
    rows = ref[:, block * sensors : (block + 1) * sensors, :]
    return rows.reshape(rows.shape[0] * sensors, rows.shape[2])


def put_rows(ref, block, sensors, rows):
    ref[:, block * sensors : (block + 1) * sensors, :] = rows.reshape(
        ref.shape[0], sensors, rows.shape[1]
    )


def scale_of(width):
    return sharpness_divisor / width


def weigh_in(key_raw, projector):
    inverse = inverse_norm(key_raw)
    unit = key_raw * inverse
    mapping = projector * inverse_norm(projector)
    scale = scale_of(key_raw.shape[-1])
    return inverse, unit, jnp.exp(scale * close_dot(mapping, unit, 1, 1))


def in_kernel(share, sensors, swapped, projector, wk, wv, sums_ref):
    tokens, width = projector.shape
    same = diagonal(tokens)
    tail = share * tokens
    sums_ref[tail:, :] = jnp.zeros((sums_ref.shape[0] - tail, width), f32)
    both_weights = jnp.concatenate([wk[...], wv[...]], axis=1)
    steps = range(share)
    both = [dot(rows_of(swapped, t, sensors).astype(bf16), both_weights, 1, 0) for t in steps]
    weights = [weigh_in(raw[:, :width], projector[...])[2] for raw in both]
    dens = [jnp.sum(weight, axis=1, keepdims=True) for weight in weights]
    nums = [rounded_dot(weights[t], both[t][:, width:], 1, 0) for t in steps]
    for t in steps:
        sums_ref[t * tokens : (t + 1) * tokens, :] = nums[t]
        sums_ref[tail + t : tail + t + 1, :tokens] = jnp.sum(
            jnp.where(same, dens[t], 0.0), axis=0, keepdims=True
        )


def total_of(refs):
    total = refs[0][...]
    for ref in refs[1:]:
        total = total + ref[...]
    return total


def num_den(total, t, share, tokens):
    num = total[t * tokens : (t + 1) * tokens, :]
    at = share * tokens + t
    den = jnp.sum(
        jnp.where(diagonal(tokens), total[at : at + 1, :tokens], 0.0), axis=1, keepdims=True
    )
    return num, den


def ready_kernel(
    share, sensors, swapped, projector, wk, wv, wq, wo,
    in_ref, out_ref,
):
    width = wk.shape[0]
    tokens = projector.shape[0]
    together = jnp.concatenate([wk[...], wv[...], wq[...]], axis=1)
    for t in range(share):
        hidden = rows_of(swapped, t, sensors).astype(bf16)
        at = slice(t * hidden.shape[0], (t + 1) * hidden.shape[0])
        raw = dot(hidden, together, 1, 0)
        inverse, unit, weights = weigh_in(raw[:, :width], projector[...])
        query_raw = raw[:, 2 * width :]
        query_inverse = inverse_norm(query_raw)
        in_ref[0, at, :] = unit
        in_ref[1, at, :] = jnp.broadcast_to(inverse, unit.shape)
        in_ref[2, at, :] = raw[:, width : 2 * width].astype(bf16).astype(f32)
        for block in range(hidden.shape[0] // width):
            to = block * tokens + t * hidden.shape[0]
            in_ref[3, to : to + tokens, :] = weights[:, block * width : (block + 1) * width]
        out_ref[0, at, :] = query_raw * query_inverse
        out_ref[1, at, :] = jnp.broadcast_to(query_inverse, unit.shape)
        cotangent = rows_of(swapped, share + t, sensors).astype(bf16)
        out_ref[2, at, :] = dot(cotangent, wo[...], 1, 1).astype(bf16).astype(f32)


def out_kernel(share, terms, ready_ref, *refs):
    sums, (ds_ref, normed_ref, d_scores_ref) = refs[:terms], refs[terms:]
    width = ready_ref.shape[2]
    tokens = ds_ref.shape[0] // share
    scale = scale_of(width)
    total = total_of(sums)
    n_rows = ready_ref.shape[1] // share
    steps = range(share)
    units = [ready_ref[0, t * n_rows : (t + 1) * n_rows, :] for t in steps]
    summaries = []
    for t in steps:
        num, den = num_den(total, t, share, tokens)
        summaries.append(num / den)
    inverses = [inverse_norm(summary) for summary in summaries]
    pooled = [summary * inverse for summary, inverse in zip(summaries, inverses)]
    weights = [jnp.exp(scale * close_dot(pooled[t], units[t], 1, 1)) for t in steps]
    attention = [weight / jnp.sum(weight, axis=0, keepdims=True) for weight in weights]
    blended = [rounded_dot(attention[t], summaries[t], 0, 0) for t in steps]
    blended_inverses = [inverse_norm(each) for each in blended]
    normed = [each * inverse for each, inverse in zip(blended, blended_inverses)]
    d_blended = [
        normalize_back(
            blended_inverses[t], normed[t], ready_ref[2, t * n_rows : (t + 1) * n_rows, :]
        )
        for t in steps
    ]
    d_attention = [close_dot(summaries[t], d_blended[t], 1, 1) for t in steps]
    d_scores = [
        attention[t]
        * (d_attention[t] - jnp.sum(attention[t] * d_attention[t], axis=0, keepdims=True))
        for t in steps
    ]
    d_pooled = [scale * rounded_dot(d_scores[t], units[t], 1, 0) for t in steps]
    direct = [close_dot(attention[t], d_blended[t], 1, 0) for t in steps]
    for t in steps:
        own = slice(t * tokens, (t + 1) * tokens)
        ds_ref[own, :] = direct[t] + normalize_back(inverses[t], pooled[t], d_pooled[t])
        d_scores_ref[own, :] = d_scores[t]
        normed_ref[t * n_rows : (t + 1) * n_rows, :] = normed[t].astype(bf16)


def query_kernel(share, sensors, terms, swapped, wq, wo, ready_ref, normed_ref, d_scores_ref, *refs):
    sums, (lay_ref, dh_ref) = refs[:terms], refs[terms:]
    width = wq.shape[0]
    tokens = d_scores_ref.shape[0] // share
    scale = scale_of(width)
    total = total_of(sums)
    n_rows = ready_ref.shape[1] // share
    grad_rows = share * n_rows
    for t in range(share):
        at = slice(t * n_rows, (t + 1) * n_rows)
        rows = rows_of(swapped, t, sensors)
        cotangent = rows_of(swapped, share + t, sensors)
        normed = normed_ref[at, :]
        layer = (rows + dot(normed, wo[...], 1, 0)).astype(bf16).astype(f32)
        put_rows(lay_ref, t, sensors, layer)
        grad_out = dot(normed, cotangent.astype(bf16), 0, 0)
        num, den = num_den(total, t, share, tokens)
        summary = num / den
        pooled = summary * inverse_norm(summary)
        d_unit = scale * close_dot(d_scores_ref[t * tokens : (t + 1) * tokens, :], pooled, 0, 0)
        d_query = normalize_back(ready_ref[1, at, :], ready_ref[0, at, :], d_unit).astype(bf16)
        grad_query = dot(rows.astype(bf16), d_query, 0, 0)
        dh_ref[at, :] = cotangent + dot(d_query, wq[...], 1, 1)
        for i, grad in enumerate((grad_query, grad_out)):
            to = slice(grad_rows + i * width, grad_rows + (i + 1) * width)
            dh_ref[to, :] = grad if t == 0 else dh_ref[to, :] + grad


def put_partials(ref, grads):
    owners, rows, width = ref.shape
    for m in range(owners):
        at = 0
        for grad in grads:
            own = grad.shape[0] // owners
            ref[m, at : at + own, :] = grad[m * own : (m + 1) * own, :]
            at += own
        if at < rows:
            ref[m, at:, :] = jnp.zeros((rows - at, width), f32)


def in_back_kernel(
    share, sensors, terms, swapped, projector, wk, wv, ready_ref, dh_ref, layer_ref, *refs
):
    sums, d_sums = refs[:terms], refs[terms : 2 * terms]
    far_ref, part_ref, out_ref, sems = refs[2 * terms :]
    half = share * sensors
    sent = [pltpu.make_async_copy(layer_ref, far_ref.at[:, pl.ds(0, half)], sems.at[share])]
    sent[0].start()
    tokens, width = projector.shape
    scale = scale_of(width)
    total = total_of(sums)
    d_total = total_of(d_sums)
    mapping_inverse = inverse_norm(projector[...])
    mapping = projector[...] * mapping_inverse
    turned = jnp.concatenate([wk[...], wv[...]], axis=1)
    n_rows = ready_ref.shape[1] // share
    grad_rows = share * n_rows
    steps = range(share)
    spans = [slice(t * n_rows, (t + 1) * n_rows) for t in steps]
    hidden = [rows_of(swapped, t, sensors).astype(bf16) for t in steps]
    units = [ready_ref[0, span, :] for span in spans]
    weights = [
        jnp.concatenate(
            [
                ready_ref[3, t * n_rows + i * tokens : t * n_rows + (i + 1) * tokens, :]
                for i in range(n_rows // width)
            ],
            axis=1,
        )
        for t in steps
    ]
    d_nums, d_dens = [], []
    for t in steps:
        num, den = num_den(total, t, share, tokens)
        d_summary = d_total[t * tokens : (t + 1) * tokens, :]
        d_nums.append(d_summary / den)
        d_dens.append(-jnp.sum(d_summary * num, axis=1, keepdims=True) / (den * den))
    d_weights = []
    for t in steps:
        high, low = split(d_nums[t])
        values = ready_ref[2, spans[t], :].astype(bf16)
        d_weights.append(dot(high, values, 1, 1) + dot(low, values, 1, 1) + d_dens[t])
    d_scores = [d_weights[t] * weights[t] for t in steps]
    d_units = [scale * rounded_dot(d_scores[t], mapping, 0, 0) for t in steps]
    d_values = [rounded_dot(weights[t], d_nums[t], 0, 0).astype(bf16) for t in steps]
    d_keys = [
        normalize_back(ready_ref[1, spans[t], :], units[t], d_units[t]).astype(bf16) for t in steps
    ]
    together = [jnp.concatenate([d_keys[t], d_values[t]], axis=1) for t in steps]
    for t in steps:
        put_rows(out_ref, t, sensors, dh_ref[spans[t], :] + dot(together[t], turned, 1, 1))
        copy = pltpu.make_async_copy(
            out_ref.at[:, pl.ds(t * sensors, sensors)],
            far_ref.at[:, pl.ds(half + t * sensors, sensors)],
            sems.at[t],
        )
        copy.start()
        sent.append(copy)
    d_mapping = sum(scale * rounded_dot(d_scores[t], units[t], 1, 0) for t in steps)
    gradients = sum(dot(hidden[t], together[t], 0, 0) for t in steps)
    parts = [normalize_back(mapping_inverse, mapping, d_mapping)]
    parts += [gradients[:, :width], gradients[:, width:]]
    parts += [dh_ref[grad_rows + i * width : grad_rows + (i + 1) * width, :] for i in range(2)]
    put_partials(part_ref, parts)
    for copy in sent:
        copy.wait()


def deal_kernel(count, place_ref, *refs):
    chunks, out_refs, rows = refs[:count], refs[count:-1], refs[-1]
    for m, chunk in enumerate(chunks):
        source = lax.bitwise_xor(place_ref[0], m)
        rows[pl.ds(source * chunk.shape[0], chunk.shape[0]), :] = chunk[...]
    at = 0
    for out in out_refs:
        out[...] = rows[at : at + out.shape[0], :]
        at += out.shape[0]


def call(kernel, out_shape, *args, vmem=32, **more):
    return pl.pallas_call(kernel, out_shape=out_shape, compiler_params=params(vmem), **more)(*args)


def group_size(most, *sizes):
    group = 1
    while group < most and all(size % (2 * group) == 0 for size in sizes):
        group *= 2
    return group


def per_device(n_sensor, n_tm, inputs, mask, projector, w_key, w_value, w_query, w_out, cotangent):
    sensors, steps, width = inputs.shape
    tokens = projector.shape[0]
    group = group_size(8, n_sensor, steps)
    rest = n_sensor // group
    share = steps // group
    blocks = [list(range(r * group, (r + 1) * group)) for r in range(rest)]

    def swap(rows):
        return lax.all_to_all(rows, "sensor", 0, 0, tiled=True, axis_index_groups=blocks)

    def others(rows):
        return [
            lax.ppermute(
                rows, "sensor", [(i, (i + step * group) % n_sensor) for i in range(n_sensor)]
            )
            for step in range(1, rest)
        ]

    def shape(*dims, kind=f32):
        return jax.ShapeDtypeStruct(dims, kind)

    wide = pltpu.VMEM(inputs.shape, f32)
    mask = mask.T

    place_spec = pl.BlockSpec(memory_space=pltpu.SMEM)
    far_spec = pl.BlockSpec(memory_space=pltpu.HBM)
    near_spec = pl.BlockSpec(memory_space=pltpu.VMEM)
    swapped = swap(
        call(
            outward_kernel,
            shape(group, 2 * share * sensors, width),
            inputs, mask, cotangent,
            vmem=60,
            in_specs=[far_spec, far_spec, far_spec],
            out_specs=far_spec,
            scratch_shapes=[
                pltpu.VMEM(inputs.shape, bf16),
                pltpu.VMEM(mask.shape, mask.dtype),
                pltpu.VMEM(inputs.shape, bf16),
                wide,
                pltpu.VMEM((group, 2 * share * sensors, width), f32),
                pltpu.SemaphoreType.DMA((2 * group + 3,)),
            ],
        )
    )
    n_rows = group * sensors
    sums_rows = share * tokens + -(-share // 8) * 8
    sums = call(
        functools.partial(in_kernel, share, sensors),
        shape(sums_rows, width),
        swapped, projector, w_key, w_value,
    )
    sums = [sums] + others(sums)
    tokens_shape = shape(share * tokens, n_rows)
    owned = [tokens // n_tm] + [width // n_tm] * 4
    quarter = group_size(4, n_sensor)
    chunk = -(-sum(owned) // (8 * quarter)) * 8
    ready_in, ready_out = call(
        functools.partial(ready_kernel, share, sensors),
        (shape(4, share * n_rows, width), shape(3, share * n_rows, width)),
        swapped, projector, w_key, w_value, w_query, w_out,
    )
    d_sums, normed, d_scores = call(
        functools.partial(out_kernel, share, rest),
        (shape(share * tokens, width), shape(share * n_rows, width, kind=bf16), tokens_shape),
        ready_out, *sums,
    )
    d_sums = [d_sums] + others(d_sums)
    layer, d_hidden = call(
        functools.partial(query_kernel, share, sensors, rest),
        (
            shape(group, share * sensors, width),
            shape(share * n_rows + 2 * width, width),
        ),
        swapped, w_query, w_out, ready_out, normed, d_scores, *sums,
    )
    back, part = call(
        functools.partial(in_back_kernel, share, sensors, rest),
        (
            shape(group, 2 * share * sensors, width),
            shape(n_tm, quarter * chunk, width),
        ),
        swapped, projector, w_key, w_value, ready_in, d_hidden, layer, *sums, *d_sums,
        out_specs=(far_spec, near_spec),
        scratch_shapes=[
            pltpu.VMEM((group, share * sensors, width), f32),
            pltpu.SemaphoreType.DMA((share + 1,)),
        ],
    )
    me = lax.axis_index("tm")
    mine = lax.dynamic_index_in_dim(part, me, 0, keepdims=False)
    for step in range(1, n_tm):
        gone = lax.dynamic_index_in_dim(part, lax.rem(me + step, n_tm), 0, keepdims=False)
        ring = [(i, (i + step) % n_tm) for i in range(n_tm)]
        mine = mine + lax.ppermute(gone, "tm", ring)

    def partner(rows, m):
        return lax.ppermute(rows, "sensor", [(i, i ^ m) for i in range(n_sensor)])

    mine = mine.reshape(quarter, chunk, width)
    place = lax.rem(lax.axis_index("sensor"), quarter)
    total = lax.dynamic_index_in_dim(mine, place, 0, keepdims=False)
    for m in range(1, quarter):
        gone = lax.dynamic_index_in_dim(mine, lax.bitwise_xor(place, m), 0, keepdims=False)
        total = total + partner(gone, m)
    home = swap(back)
    output_rows, d_inputs = call(
        homeward_kernel,
        (shape(*inputs.shape, kind=bf16), shape(*inputs.shape, kind=bf16)),
        home, mask,
        scratch_shapes=[wide, wide],
    )
    m = quarter
    while n_sensor % (2 * m) == 0:
        gone = partner(total, m)
        m *= 2
        if n_sensor % (2 * m):
            total, gone, output_rows, d_inputs = lax.optimization_barrier(
                (total, gone, output_rows, d_inputs)
            )
        total = total + gone
    odd = n_sensor // m
    spread = [
        lax.ppermute(total, "sensor", [(i, (i + step * m) % n_sensor) for i in range(n_sensor)])
        for step in range(1, odd)
    ]
    total = sum(spread, total)
    chunks = [total] + [partner(total, m) for m in range(1, quarter)]
    outs = call(
        functools.partial(deal_kernel, quarter),
        tuple(shape(n, width) for n in owned),
        place[None], *chunks,
        in_specs=[place_spec] + [near_spec] * quarter,
        scratch_shapes=[pltpu.VMEM((quarter * chunk, width), f32)],
    )
    return (output_rows, d_inputs, *outs)


def solution(mesh):
    placed = (
        P("sensor", "tm", None),
        P("sensor", "tm"),
        P(),
        P(),
        P(),
        P(),
        P(),
        P("sensor", "tm", None),
    )
    return jax.shard_map(
        functools.partial(per_device, mesh.shape["sensor"], mesh.shape["tm"]),
        mesh=mesh,
        in_specs=placed,
        out_specs=(
            P("sensor", "tm", None),
            P("sensor", "tm", None),
            P("tm", None),
            P("tm", None),
            P("tm", None),
            P("tm", None),
            P("tm", None),
        ),
        check_vma=False,
    )
```

```python
import functools

import jax
import jax.numpy as jnp
from jax import lax
from jax.experimental import pallas as pl
from jax.experimental.pallas import tpu as pltpu
from jax.sharding import PartitionSpec as P

sharpness_divisor = 12.0
epsilon = 1e-06
f32 = jnp.float32
bf16 = jnp.bfloat16


def params(mebibytes=32):
    return pltpu.CompilerParams(vmem_limit_bytes=mebibytes * 1024 * 1024)


def dot(left, right, left_dim, right_dim):
    return lax.dot_general(
        left, right, (((left_dim,), (right_dim,)), ((), ())), preferred_element_type=f32
    )


def rounded_dot(left, right, left_dim, right_dim):
    return dot(left.astype(bf16), right.astype(bf16), left_dim, right_dim)


def split(value):
    high = value.astype(bf16)
    return high, (value - high.astype(f32)).astype(bf16)


def close_dot(left, right, left_dim, right_dim):
    high, low = split(left)
    right_high, right_low = split(right)
    return dot(
        jnp.concatenate([high, high, low], axis=left_dim),
        jnp.concatenate([right_high, right_low, right_high], axis=right_dim),
        left_dim,
        right_dim,
    )


def inverse_norm(vector):
    return lax.rsqrt(jnp.mean(vector * vector, axis=-1, keepdims=True) + epsilon)


def normalize_back(inverse, unit, gradient):
    return inverse * (gradient - unit * jnp.mean(unit * gradient, axis=-1, keepdims=True))


def diagonal(tokens):
    rows = lax.broadcasted_iota(jnp.int32, (tokens, tokens), 0)
    return rows == lax.broadcasted_iota(jnp.int32, (tokens, tokens), 1)


def turned_mask(mask_ref):
    sensors = mask_ref.shape[1]
    return dot(diagonal(sensors).astype(f32).astype(bf16), mask_ref[...].astype(f32).astype(bf16), 1, 1)


def outward_kernel(
    inputs_ref, mask_ref, cotangent_ref, far_ref, near, near_mask, near_cotangent, wide, out_ref, sems
):
    sensors, steps, _ = inputs_ref.shape
    places = out_ref.shape[0]
    share = steps // places
    rows = share * sensors
    first = pltpu.make_async_copy(inputs_ref, near, sems.at[2 * places])
    second = pltpu.make_async_copy(cotangent_ref, near_cotangent, sems.at[2 * places + 1])
    third = pltpu.make_async_copy(mask_ref, near_mask, sems.at[2 * places + 2])
    first.start()
    third.start()
    second.start()
    sent = []

    def send(place, half):
        block = (place, pl.ds(half * rows, rows))
        copy = pltpu.make_async_copy(
            out_ref.at[block], far_ref.at[block], sems.at[half * places + place]
        )
        copy.start()
        sent.append(copy)

    third.wait()
    marks = turned_mask(near_mask)
    first.wait()
    wide[...] = near[...].astype(f32)
    for place in range(places):
        for own in range(share):
            t = place * share + own
            out_ref[place, own * sensors : (own + 1) * sensors, :] = (
                wide[:, t, :] * marks[:, t : t + 1]
            )
        send(place, 0)
    second.wait()
    wide[...] = near_cotangent[...].astype(f32)
    for place in range(places):
        for own in range(share):
            at = rows + own * sensors
            out_ref[place, at : at + sensors, :] = wide[:, place * share + own, :]
        send(place, 1)
    for copy in sent:
        copy.wait()


def homeward_kernel(rows_ref, mask_ref, layer_ref, d_inputs_ref, wide, wide_gradient):
    sensors, steps, _ = layer_ref.shape
    share = steps // rows_ref.shape[0]
    marks = turned_mask(mask_ref)
    for t in range(steps):
        place, own = divmod(t, share)
        wide[:, t, :] = rows_ref[place, own * sensors : (own + 1) * sensors, :]
        at = (share + own) * sensors
        wide_gradient[:, t, :] = rows_ref[place, at : at + sensors, :] * marks[:, t : t + 1]
    layer_ref[...] = wide[...].astype(bf16)
    d_inputs_ref[...] = wide_gradient[...].astype(bf16)


def rows_of(ref, block, sensors):
    rows = ref[:, block * sensors : (block + 1) * sensors, :]
    return rows.reshape(rows.shape[0] * sensors, rows.shape[2])


def put_rows(ref, block, sensors, rows):
    ref[:, block * sensors : (block + 1) * sensors, :] = rows.reshape(
        ref.shape[0], sensors, rows.shape[1]
    )


def scale_of(width):
    return sharpness_divisor / width


def weigh_in(key_raw, projector):
    inverse = inverse_norm(key_raw)
    unit = key_raw * inverse
    mapping = projector * inverse_norm(projector)
    scale = scale_of(key_raw.shape[-1])
    return inverse, unit, jnp.exp(scale * close_dot(mapping, unit, 1, 1))


def in_kernel(share, sensors, swapped, projector, wk, wv, sums_ref):
    tokens, width = projector.shape
    same = diagonal(tokens)
    tail = share * tokens
    sums_ref[tail:, :] = jnp.zeros((sums_ref.shape[0] - tail, width), f32)
    both_weights = jnp.concatenate([wk[...], wv[...]], axis=1)
    steps = range(share)
    both = [dot(rows_of(swapped, t, sensors).astype(bf16), both_weights, 1, 0) for t in steps]
    weights = [weigh_in(raw[:, :width], projector[...])[2] for raw in both]
    dens = [jnp.sum(weight, axis=1, keepdims=True) for weight in weights]
    nums = [rounded_dot(weights[t], both[t][:, width:], 1, 0) for t in steps]
    for t in steps:
        sums_ref[t * tokens : (t + 1) * tokens, :] = nums[t]
        sums_ref[tail + t : tail + t + 1, :tokens] = jnp.sum(
            jnp.where(same, dens[t], 0.0), axis=0, keepdims=True
        )


def total_of(refs):
    total = refs[0][...]
    for ref in refs[1:]:
        total = total + ref[...]
    return total


def num_den(total, t, share, tokens):
    num = total[t * tokens : (t + 1) * tokens, :]
    at = share * tokens + t
    den = jnp.sum(
        jnp.where(diagonal(tokens), total[at : at + 1, :tokens], 0.0), axis=1, keepdims=True
    )
    return num, den


def ready_kernel(
    share, sensors, swapped, projector, wk, wv, wq, wo,
    in_ref, out_ref,
):
    width = wk.shape[0]
    tokens = projector.shape[0]
    together = jnp.concatenate([wk[...], wv[...], wq[...]], axis=1)
    for t in range(share):
        hidden = rows_of(swapped, t, sensors).astype(bf16)
        at = slice(t * hidden.shape[0], (t + 1) * hidden.shape[0])
        raw = dot(hidden, together, 1, 0)
        inverse, unit, weights = weigh_in(raw[:, :width], projector[...])
        query_raw = raw[:, 2 * width :]
        query_inverse = inverse_norm(query_raw)
        in_ref[0, at, :] = unit
        in_ref[1, at, :] = jnp.broadcast_to(inverse, unit.shape)
        in_ref[2, at, :] = raw[:, width : 2 * width].astype(bf16).astype(f32)
        for block in range(hidden.shape[0] // width):
            to = block * tokens + t * hidden.shape[0]
            in_ref[3, to : to + tokens, :] = weights[:, block * width : (block + 1) * width]
        out_ref[0, at, :] = query_raw * query_inverse
        out_ref[1, at, :] = jnp.broadcast_to(query_inverse, unit.shape)
        cotangent = rows_of(swapped, share + t, sensors).astype(bf16)
        out_ref[2, at, :] = dot(cotangent, wo[...], 1, 1).astype(bf16).astype(f32)


def out_kernel(share, terms, ready_ref, *refs):
    sums, (ds_ref, normed_ref, d_scores_ref) = refs[:terms], refs[terms:]
    width = ready_ref.shape[2]
    tokens = ds_ref.shape[0] // share
    scale = scale_of(width)
    total = total_of(sums)
    n_rows = ready_ref.shape[1] // share
    steps = range(share)
    units = [ready_ref[0, t * n_rows : (t + 1) * n_rows, :] for t in steps]
    summaries = []
    for t in steps:
        num, den = num_den(total, t, share, tokens)
        summaries.append(num / den)
    inverses = [inverse_norm(summary) for summary in summaries]
    pooled = [summary * inverse for summary, inverse in zip(summaries, inverses)]
    weights = [jnp.exp(scale * close_dot(pooled[t], units[t], 1, 1)) for t in steps]
    attention = [weight / jnp.sum(weight, axis=0, keepdims=True) for weight in weights]
    blended = [rounded_dot(attention[t], summaries[t], 0, 0) for t in steps]
    blended_inverses = [inverse_norm(each) for each in blended]
    normed = [each * inverse for each, inverse in zip(blended, blended_inverses)]
    d_blended = [
        normalize_back(
            blended_inverses[t], normed[t], ready_ref[2, t * n_rows : (t + 1) * n_rows, :]
        )
        for t in steps
    ]
    d_attention = [close_dot(summaries[t], d_blended[t], 1, 1) for t in steps]
    d_scores = [
        attention[t]
        * (d_attention[t] - jnp.sum(attention[t] * d_attention[t], axis=0, keepdims=True))
        for t in steps
    ]
    d_pooled = [scale * rounded_dot(d_scores[t], units[t], 1, 0) for t in steps]
    direct = [close_dot(attention[t], d_blended[t], 1, 0) for t in steps]
    for t in steps:
        own = slice(t * tokens, (t + 1) * tokens)
        ds_ref[own, :] = direct[t] + normalize_back(inverses[t], pooled[t], d_pooled[t])
        d_scores_ref[own, :] = d_scores[t]
        normed_ref[t * n_rows : (t + 1) * n_rows, :] = normed[t].astype(bf16)


def query_kernel(share, sensors, terms, swapped, wq, wo, ready_ref, normed_ref, d_scores_ref, *refs):
    sums, (lay_ref, dh_ref) = refs[:terms], refs[terms:]
    width = wq.shape[0]
    tokens = d_scores_ref.shape[0] // share
    scale = scale_of(width)
    total = total_of(sums)
    n_rows = ready_ref.shape[1] // share
    grad_rows = share * n_rows
    for t in range(share):
        at = slice(t * n_rows, (t + 1) * n_rows)
        rows = rows_of(swapped, t, sensors)
        cotangent = rows_of(swapped, share + t, sensors)
        normed = normed_ref[at, :]
        layer = (rows + dot(normed, wo[...], 1, 0)).astype(bf16).astype(f32)
        put_rows(lay_ref, t, sensors, layer)
        grad_out = dot(normed, cotangent.astype(bf16), 0, 0)
        num, den = num_den(total, t, share, tokens)
        summary = num / den
        pooled = summary * inverse_norm(summary)
        d_unit = scale * close_dot(d_scores_ref[t * tokens : (t + 1) * tokens, :], pooled, 0, 0)
        d_query = normalize_back(ready_ref[1, at, :], ready_ref[0, at, :], d_unit).astype(bf16)
        grad_query = dot(rows.astype(bf16), d_query, 0, 0)
        dh_ref[at, :] = cotangent + dot(d_query, wq[...], 1, 1)
        for i, grad in enumerate((grad_query, grad_out)):
            to = slice(grad_rows + i * width, grad_rows + (i + 1) * width)
            dh_ref[to, :] = grad if t == 0 else dh_ref[to, :] + grad


def put_partials(ref, grads):
    owners, rows, width = ref.shape
    for m in range(owners):
        at = 0
        for grad in grads:
            own = grad.shape[0] // owners
            ref[m, at : at + own, :] = grad[m * own : (m + 1) * own, :]
            at += own
        if at < rows:
            ref[m, at:, :] = jnp.zeros((rows - at, width), f32)


def in_back_kernel(
    share, sensors, terms, swapped, projector, wk, wv, ready_ref, dh_ref, layer_ref, *refs
):
    sums, d_sums = refs[:terms], refs[terms : 2 * terms]
    far_ref, part_ref, out_ref, sems = refs[2 * terms :]
    half = share * sensors
    sent = [pltpu.make_async_copy(layer_ref, far_ref.at[:, pl.ds(0, half)], sems.at[share])]
    sent[0].start()
    tokens, width = projector.shape
    scale = scale_of(width)
    total = total_of(sums)
    d_total = total_of(d_sums)
    mapping_inverse = inverse_norm(projector[...])
    mapping = projector[...] * mapping_inverse
    turned = jnp.concatenate([wk[...], wv[...]], axis=1)
    n_rows = ready_ref.shape[1] // share
    grad_rows = share * n_rows
    steps = range(share)
    spans = [slice(t * n_rows, (t + 1) * n_rows) for t in steps]
    hidden = [rows_of(swapped, t, sensors).astype(bf16) for t in steps]
    units = [ready_ref[0, span, :] for span in spans]
    weights = [
        jnp.concatenate(
            [
                ready_ref[3, t * n_rows + i * tokens : t * n_rows + (i + 1) * tokens, :]
                for i in range(n_rows // width)
            ],
            axis=1,
        )
        for t in steps
    ]
    d_nums, d_dens = [], []
    for t in steps:
        num, den = num_den(total, t, share, tokens)
        d_summary = d_total[t * tokens : (t + 1) * tokens, :]
        d_nums.append(d_summary / den)
        d_dens.append(-jnp.sum(d_summary * num, axis=1, keepdims=True) / (den * den))
    d_weights = []
    for t in steps:
        high, low = split(d_nums[t])
        values = ready_ref[2, spans[t], :].astype(bf16)
        parts = jnp.concatenate([high, low], axis=1)
        twice = jnp.concatenate([values, values], axis=1)
        d_weights.append(dot(parts, twice, 1, 1) + d_dens[t])
    d_scores = [d_weights[t] * weights[t] for t in steps]
    d_units = [scale * rounded_dot(d_scores[t], mapping, 0, 0) for t in steps]
    d_values = [rounded_dot(weights[t], d_nums[t], 0, 0).astype(bf16) for t in steps]
    d_keys = [
        normalize_back(ready_ref[1, spans[t], :], units[t], d_units[t]).astype(bf16) for t in steps
    ]
    together = [jnp.concatenate([d_keys[t], d_values[t]], axis=1) for t in steps]
    for t in steps:
        put_rows(out_ref, t, sensors, dh_ref[spans[t], :] + dot(together[t], turned, 1, 1))
        copy = pltpu.make_async_copy(
            out_ref.at[:, pl.ds(t * sensors, sensors)],
            far_ref.at[:, pl.ds(half + t * sensors, sensors)],
            sems.at[t],
        )
        copy.start()
        sent.append(copy)
    d_mapping = sum(scale * rounded_dot(d_scores[t], units[t], 1, 0) for t in steps)
    gradients = sum(dot(hidden[t], together[t], 0, 0) for t in steps)
    parts = [normalize_back(mapping_inverse, mapping, d_mapping)]
    parts += [gradients[:, :width], gradients[:, width:]]
    parts += [dh_ref[grad_rows + i * width : grad_rows + (i + 1) * width, :] for i in range(2)]
    put_partials(part_ref, parts)
    for copy in sent:
        copy.wait()


def deal_kernel(count, place_ref, *refs):
    chunks, out_refs, rows = refs[:count], refs[count:-1], refs[-1]
    for m, chunk in enumerate(chunks):
        source = lax.bitwise_xor(place_ref[0], m)
        rows[pl.ds(source * chunk.shape[0], chunk.shape[0]), :] = chunk[...]
    at = 0
    for out in out_refs:
        out[...] = rows[at : at + out.shape[0], :]
        at += out.shape[0]


def call(kernel, out_shape, *args, vmem=32, **more):
    return pl.pallas_call(kernel, out_shape=out_shape, compiler_params=params(vmem), **more)(*args)


def group_size(most, *sizes):
    group = 1
    while group < most and all(size % (2 * group) == 0 for size in sizes):
        group *= 2
    return group


def per_device(n_sensor, n_tm, inputs, mask, projector, w_key, w_value, w_query, w_out, cotangent):
    sensors, steps, width = inputs.shape
    tokens = projector.shape[0]
    group = group_size(8, n_sensor, steps)
    rest = n_sensor // group
    share = steps // group
    blocks = [list(range(r * group, (r + 1) * group)) for r in range(rest)]

    def swap(rows):
        return lax.all_to_all(rows, "sensor", 0, 0, tiled=True, axis_index_groups=blocks)

    def others(rows):
        return [
            lax.ppermute(
                rows, "sensor", [(i, (i + step * group) % n_sensor) for i in range(n_sensor)]
            )
            for step in range(1, rest)
        ]

    def shape(*dims, kind=f32):
        return jax.ShapeDtypeStruct(dims, kind)

    wide = pltpu.VMEM(inputs.shape, f32)
    mask = mask.T

    place_spec = pl.BlockSpec(memory_space=pltpu.SMEM)
    far_spec = pl.BlockSpec(memory_space=pltpu.HBM)
    near_spec = pl.BlockSpec(memory_space=pltpu.VMEM)
    swapped = swap(
        call(
            outward_kernel,
            shape(group, 2 * share * sensors, width),
            inputs, mask, cotangent,
            vmem=60,
            in_specs=[far_spec, far_spec, far_spec],
            out_specs=far_spec,
            scratch_shapes=[
                pltpu.VMEM(inputs.shape, bf16),
                pltpu.VMEM(mask.shape, mask.dtype),
                pltpu.VMEM(inputs.shape, bf16),
                wide,
                pltpu.VMEM((group, 2 * share * sensors, width), f32),
                pltpu.SemaphoreType.DMA((2 * group + 3,)),
            ],
        )
    )
    n_rows = group * sensors
    sums_rows = share * tokens + -(-share // 8) * 8
    sums = call(
        functools.partial(in_kernel, share, sensors),
        shape(sums_rows, width),
        swapped, projector, w_key, w_value,
    )
    sums = [sums] + others(sums)
    tokens_shape = shape(share * tokens, n_rows)
    owned = [tokens // n_tm] + [width // n_tm] * 4
    quarter = group_size(4, n_sensor)
    chunk = -(-sum(owned) // (8 * quarter)) * 8
    ready_in, ready_out = call(
        functools.partial(ready_kernel, share, sensors),
        (shape(4, share * n_rows, width), shape(3, share * n_rows, width)),
        swapped, projector, w_key, w_value, w_query, w_out,
    )
    d_sums, normed, d_scores = call(
        functools.partial(out_kernel, share, rest),
        (shape(share * tokens, width), shape(share * n_rows, width, kind=bf16), tokens_shape),
        ready_out, *sums,
    )
    d_sums = [d_sums] + others(d_sums)
    layer, d_hidden = call(
        functools.partial(query_kernel, share, sensors, rest),
        (
            shape(group, share * sensors, width),
            shape(share * n_rows + 2 * width, width),
        ),
        swapped, w_query, w_out, ready_out, normed, d_scores, *sums,
    )
    back, part = call(
        functools.partial(in_back_kernel, share, sensors, rest),
        (
            shape(group, 2 * share * sensors, width),
            shape(n_tm, quarter * chunk, width),
        ),
        swapped, projector, w_key, w_value, ready_in, d_hidden, layer, *sums, *d_sums,
        out_specs=(far_spec, near_spec),
        scratch_shapes=[
            pltpu.VMEM((group, share * sensors, width), f32),
            pltpu.SemaphoreType.DMA((share + 1,)),
        ],
    )
    me = lax.axis_index("tm")
    mine = lax.dynamic_index_in_dim(part, me, 0, keepdims=False)
    for step in range(1, n_tm):
        gone = lax.dynamic_index_in_dim(part, lax.rem(me + step, n_tm), 0, keepdims=False)
        ring = [(i, (i + step) % n_tm) for i in range(n_tm)]
        mine = mine + lax.ppermute(gone, "tm", ring)

    def partner(rows, m):
        return lax.ppermute(rows, "sensor", [(i, i ^ m) for i in range(n_sensor)])

    mine = mine.reshape(quarter, chunk, width)
    place = lax.rem(lax.axis_index("sensor"), quarter)
    total = lax.dynamic_index_in_dim(mine, place, 0, keepdims=False)
    for m in range(1, quarter):
        gone = lax.dynamic_index_in_dim(mine, lax.bitwise_xor(place, m), 0, keepdims=False)
        total = total + partner(gone, m)
    home = swap(back)
    output_rows, d_inputs = call(
        homeward_kernel,
        (shape(*inputs.shape, kind=bf16), shape(*inputs.shape, kind=bf16)),
        home, mask,
        scratch_shapes=[wide, wide],
    )
    m = quarter
    while n_sensor % (2 * m) == 0:
        gone = partner(total, m)
        m *= 2
        if n_sensor % (2 * m):
            total, gone, output_rows, d_inputs = lax.optimization_barrier(
                (total, gone, output_rows, d_inputs)
            )
        total = total + gone
    odd = n_sensor // m
    spread = [
        lax.ppermute(total, "sensor", [(i, (i + step * m) % n_sensor) for i in range(n_sensor)])
        for step in range(1, odd)
    ]
    total = sum(spread, total)
    chunks = [total] + [partner(total, m) for m in range(1, quarter)]
    outs = call(
        functools.partial(deal_kernel, quarter),
        tuple(shape(n, width) for n in owned),
        place[None], *chunks,
        in_specs=[place_spec] + [near_spec] * quarter,
        scratch_shapes=[pltpu.VMEM((quarter * chunk, width), f32)],
    )
    return (output_rows, d_inputs, *outs)


def solution(mesh):
    placed = (
        P("sensor", "tm", None),
        P("sensor", "tm"),
        P(),
        P(),
        P(),
        P(),
        P(),
        P("sensor", "tm", None),
    )
    return jax.shard_map(
        functools.partial(per_device, mesh.shape["sensor"], mesh.shape["tm"]),
        mesh=mesh,
        in_specs=placed,
        out_specs=(
            P("sensor", "tm", None),
            P("sensor", "tm", None),
            P("tm", None),
            P("tm", None),
            P("tm", None),
            P("tm", None),
            P("tm", None),
        ),
        check_vma=False,
    )
```
